32 devices in a mesh: dp: 2 (over x), head: 4 (over z), frame: 4 (over y, core).
Axes of the slice: x: 2, y: 2, z: 4, core: 2. Of those that a mesh axis runs over, the one named last changes fastest.
Arguments:
- queries: bfloat16 [2048, 5120], P(('dp', 'frame', 'head')), parts along dimension 0, may hold values from -5 to 5
- keys: bfloat16 [2048, 5120], P(('dp', 'frame', 'head')), parts along dimension 0, may hold values from -5 to 5
- values: bfloat16 [2048, 5120], P(('dp', 'frame', 'head')), parts along dimension 0, may hold values from -6 to 6
- out_grad: bfloat16 [2048, 5120], P(('dp', 'frame', 'head')), parts along dimension 0, may hold values from -6 to 6
- tile_mask: int32 [40, 8, 8], P('head'), may hold values from 0 to 1, as said below
Outputs:
- attended: bfloat16 [2048, 5120], P(('dp', 'frame'), 'head'), parts along dimension 0
- query_grad: bfloat16 [2048, 5120], P(('dp', 'frame'), 'head'), parts along dimension 0
- key_grad: bfloat16 [2048, 5120], P(('dp', 'frame'), 'head'), parts along dimension 0
- value_grad: bfloat16 [2048, 5120], P(('dp', 'frame'), 'head'), parts along dimension 0
The draws below stay inside these ranges and needn't reach their ends.
There are 2 independent parts, one for each index of `dp`. The reference program is written for one: setup_inputs(seed, part) draws one part's arguments, and reference() takes and returns one part's arrays. A program takes and returns all parts, laid end to end along the dimension named above; an argument that names none is the same for every part. Nothing has to cross between parts.
Inputs may be any that keep to these rules, and one draw needn't show every extreme that they name: tile_mask[h, i, i] = 1 for every head h and tile i.
All inputs are finite; a program needn't handle non-finite values.
Results may differ from the reference program's by a relative error of at most 0.022.
Values may be sent and summed in bfloat16 or wider, within the bound.
No kernel may reach another device: no remote copies, remote signals or barrier semaphores. Data moves between devices by JAX's collectives and lax.ppermute only.
A program may use at most 128 MiB of HBM per device.

```python
import math
import jax
import jax.numpy as jnp
from jax import lax

H = 40
HD = 128
D = 5120
TILE = 128
SLAB = 256
TOKENS = 1024
NB = 8


def paired_fields(key):
    base = jax.random.fold_in(key, 7)
    first, second = jax.random.split(base, 2)
    query_field = jax.random.truncated_normal(first, -4.5, 4.5, (TOKENS, D), jnp.float32)
    key_field = jax.random.truncated_normal(second, -4.5, 4.5, (TOKENS, D), jnp.float32)
    return (query_field, key_field)


def draw_queries(key, part):
    return paired_fields(key)[0].astype(jnp.bfloat16)


def draw_keys(key, part):
    return paired_fields(key)[1].astype(jnp.bfloat16)


def draw_tile_mask(key, part):
    base = jax.random.fold_in(key, 11)
    first, second = jax.random.split(base, 2)
    level = jax.random.randint(first, (H, 1, 1), 0, 6)
    threshold = jnp.left_shift(jnp.int32(1), level)
    rolls = jax.random.randint(second, (H, NB, NB), 0, 64)
    diagonal = jnp.arange(NB)[:, None] == jnp.arange(NB)[None, :]
    return jnp.where(diagonal[None, :, :] | (rolls < threshold), 1, 0).astype(jnp.int32)


def level_of(stream_key, extent, cuts, low, high):
    factor_of, own = 1.0, jax.random.fold_in(stream_key, 6)
    for dim, parts in cuts:
        draws = jnp.exp(jax.random.uniform(jax.random.fold_in(own, dim), (parts,), jnp.float32, low / len(cuts), high / len(cuts)))
        factor_of = factor_of * jnp.repeat(draws, extent[dim] // parts).reshape([-1 if axis == dim else 1 for axis in range(len(extent))])
    return factor_of


def scatter_about(stream_key, dims, spread, most, cuts=(), kind=jnp.bfloat16):
    level = level_of(stream_key, dims, cuts, -0.22, 0.18) if cuts else 1.0
    drawn = jax.random.normal(stream_key, dims, jnp.float32) * spread * level
    return jnp.minimum(jnp.maximum(drawn, -most), most).astype(kind)


def setup_inputs(seed: int = 0, part: int = 0) -> dict:
    key_list = jax.random.split(jax.random.key(seed), 6)
    own_keys = jax.random.split(jax.random.fold_in(key_list[5], part), 6)
    return {
        "queries": draw_queries(jax.random.fold_in(jax.random.fold_in(key_list[5], part), 71), part),
        "keys": draw_keys(jax.random.fold_in(jax.random.fold_in(key_list[5], part), 71), part),
        "values": scatter_about(own_keys[2], (TOKENS, D), 1.0, 6.0, ((0, 16),)),
        "out_grad": scatter_about(own_keys[3], (TOKENS, D), 1.0, 6.0, ((0, 16),)),
        "tile_mask": draw_tile_mask(jax.random.fold_in(key_list[5], 71), part),
    }


EXCLUDED = -1e+30

def head_pass(inputs):
    query_head, key_head, value_head, grad_head, mask_head = inputs
    scaling = 1.0 / math.sqrt(HD)
    scores = jnp.dot(query_head, key_head.T, preferred_element_type=jnp.float32) * scaling
    allowed = jnp.repeat(jnp.repeat(mask_head, TILE, axis=0), TILE, axis=1) == 1
    masked = jnp.where(allowed, scores, EXCLUDED)
    peak = lax.optimization_barrier(jnp.max(masked, axis=1))
    weights = jnp.where(allowed, jnp.exp(masked - peak[:, None]), 0.0)
    totals = lax.optimization_barrier(jnp.sum(weights, axis=1))
    attended = (jnp.dot(weights.astype(jnp.bfloat16), value_head, preferred_element_type=jnp.float32) / totals[:, None]).astype(jnp.bfloat16)
    logsum = peak + jnp.log(totals)
    out_delta = lax.optimization_barrier(jnp.sum(grad_head.astype(jnp.float32) * attended.astype(jnp.float32), axis=1))
    probabilities = jnp.where(allowed, jnp.exp(masked - logsum[:, None]), 0.0)
    prob_grad = jnp.dot(grad_head, value_head.T, preferred_element_type=jnp.float32)
    score_grad = probabilities * (prob_grad - out_delta[:, None])
    probs_half = lax.optimization_barrier(probabilities.astype(jnp.bfloat16))
    score_half = lax.optimization_barrier(score_grad.astype(jnp.bfloat16))
    query_grad = (jnp.dot(score_half, key_head, preferred_element_type=jnp.float32) * scaling).astype(jnp.bfloat16)
    slab_count = TOKENS // SLAB
    grad_slabs = grad_head.astype(jnp.float32).reshape(slab_count, SLAB, HD)
    query_slabs = query_head.astype(jnp.float32).reshape(slab_count, SLAB, HD)
    value_parts = jnp.einsum('sqk,sqd->skd', probs_half.astype(jnp.float32).reshape(slab_count, SLAB, TOKENS), grad_slabs)
    value_parts = lax.optimization_barrier(value_parts.astype(jnp.bfloat16))
    value_grad = lax.optimization_barrier(jnp.sum(value_parts.astype(jnp.float32), axis=0)).astype(jnp.bfloat16)
    key_parts = jnp.einsum('sqk,sqd->skd', score_half.astype(jnp.float32).reshape(slab_count, SLAB, TOKENS), query_slabs) * scaling
    key_parts = lax.optimization_barrier(key_parts.astype(jnp.bfloat16))
    key_grad = lax.optimization_barrier(jnp.sum(key_parts.astype(jnp.float32), axis=0)).astype(jnp.bfloat16)
    return (attended, query_grad, key_grad, value_grad)

def split_heads(field):
    return field.reshape(TOKENS, H, HD).transpose(1, 0, 2)

def join_heads(field):
    return field.transpose(1, 0, 2).reshape(TOKENS, H * HD)

def reference(queries, keys, values, out_grad, tile_mask):
    results = lax.map(head_pass, (split_heads(queries), split_heads(keys), split_heads(values), split_heads(out_grad), tile_mask))
    return (join_heads(results[0]), join_heads(results[1]), join_heads(results[2]), join_heads(results[3]))
```

```python
import functools
import math

import jax
import jax.numpy as jnp
from jax import lax
from jax.experimental import pallas as pl
from jax.experimental.pallas import tpu as pltpu
from jax.sharding import PartitionSpec as P

HD = 128
TILE = 128
EXCLUDED = -1e30
LOG2E = 1.4426950408889634
F32 = jnp.float32
BF16 = jnp.bfloat16
VMEM_LIMIT = 48 * 1024 * 1024
VMEM = pl.BlockSpec(memory_space=pltpu.VMEM)
SMEM = pl.BlockSpec(memory_space=pltpu.SMEM)


def there(index, step, size):
    if size & (size - 1) == 0:
        return index ^ step
    return (index + step) % size


def back(index, step, size):
    return there(index, step if size & (size - 1) == 0 else size - step, size)


class Plan:
    def __init__(self, rows, width, head_axis, frame_axis):
        self.rows = rows
        self.zn = head_axis
        self.groups = width // HD // head_axis
        self.on = math.gcd(self.groups, frame_axis)
        self.inn = frame_axis // self.on
        self.mine = self.groups // self.on
        self.slab = rows * head_axis
        self.tq = self.slab * self.on
        self.tk = self.tq * self.inn

    def place(self):
        frame = lax.axis_index("frame")
        return lax.axis_index("head"), frame // self.inn, frame % self.inn

    def column(self, z, o, first):
        return pl.multiple_of((z * self.groups + o * self.mine + first) * HD, HD)

    def send(self, array, z_step=0, o_step=0, i_step=0, returning=False):
        go = back if returning else there
        pairs = []
        for z in range(self.zn):
            for o in range(self.on):
                for i in range(self.inn):
                    source = (z * self.on + o) * self.inn + i
                    target = (
                        go(z, z_step, self.zn) * self.on + go(o, o_step, self.on)
                    ) * self.inn + go(i, i_step, self.inn)
                    pairs.append((source, target))
        return lax.ppermute(array, ("head", "frame"), pairs)


def shape(*dims, dtype=BF16):
    return jax.ShapeDtypeStruct(dims, dtype)


def call_mover(body, operands, out_shape, name):
    total = sum(math.prod(s.shape) * 2 for s in out_shape)
    return pl.pallas_call(
        body,
        out_shape=out_shape,
        in_specs=[VMEM] * len(operands),
        out_specs=[VMEM] * len(out_shape),
        compiler_params=pltpu.CompilerParams(vmem_limit_bytes=VMEM_LIMIT),
        cost_estimate=pl.CostEstimate(flops=0, bytes_accessed=2 * total, transcendentals=0),
        name=name,
    )(*operands)


def pack_outer(plan, arrays, first, width):
    def body(*refs):
        ins, outs = refs[:4], refs[4:]
        z, o, _ = plan.place()
        for step, out in enumerate(outs, 1):
            for k in range(plan.zn):
                at = plan.column(there(z, k, plan.zn), there(o, step, plan.on), first)
                for a, ref in enumerate(ins):
                    out[k, a] = ref[:, pl.ds(at, width)]

    out = [shape(plan.zn, 4, plan.rows, width)] * (plan.on - 1)
    return call_mover(body, arrays, out, "pack_outer")


def pack_heads(plan, arrays, received, first, width):
    def body(*refs):
        ins, got = refs[:4], refs[4 : 4 + len(received)]
        z, o, _ = plan.place()
        for k, out in enumerate(refs[4 + len(received) :]):
            at = plan.column(there(z, k, plan.zn), o, first)
            for a, ref in enumerate(ins):
                out[0, a] = ref[:, pl.ds(at, width)]
            for step, ref in enumerate(got, 1):
                out[step] = ref[k]

    out = [shape(plan.on, 4, plan.rows, width)] * plan.zn
    return call_mover(body, [*arrays, *received], out, "pack_heads")


def join_rows(plan, pieces, width):
    def body(*refs):
        ins, (qg, kv) = refs[: plan.zn], refs[plan.zn :]
        z = lax.axis_index("head")
        for k, ref in enumerate(ins):
            row = back(z, k, plan.zn) * plan.rows
            for step in range(plan.on):
                at = pl.ds(pl.multiple_of(step * plan.slab + row, plan.rows), plan.rows)
                for a in range(2):
                    qg[a, at], kv[a, at] = ref[step, a], ref[step, 2 + a]

    out = [shape(2, plan.tq, width)] * 2
    return call_mover(body, pieces, out, "join_rows")


def attend_body(plan, first, heads, *refs):
    mask, qg, kvs = refs[0], refs[1], refs[2 : 2 + plan.inn]
    rest = refs[2 + plan.inn :]
    row_outs, key_outs = rest[: plan.on], rest[plan.on : plan.on + plan.inn]
    key_t, value_t, scores, weights, grads, key_acc, value_acc = rest[plan.on + plan.inn :]
    _, o, i = plan.place()
    scaling = 1.0 / math.sqrt(HD)
    slab, tiles = plan.slab, plan.slab // TILE
    nt = (((1,), (1,)), ((), ()))
    dot = functools.partial(jnp.dot, preferred_element_type=F32)
    spots = [
        (m, step, t) for m in range(plan.inn) for step in range(plan.on) for t in range(tiles)
    ]

    def one_head(h, carry):
        cols = pl.ds(pl.multiple_of(h * HD, HD), HD)
        head = o * plan.mine + first + h
        for n, (m, step, t) in enumerate(spots):
            at = pl.ds(step * slab + t * TILE, TILE)
            put = pl.ds(n * TILE, TILE)
            key_t[:, put] = kvs[m][0, at, cols].astype(F32).T.astype(BF16)
            value_t[:, put] = kvs[m][1, at, cols].astype(F32).T.astype(BF16)

        for q_step in range(plan.on):
            q_at = pl.ds(q_step * slab, slab)
            q, g = qg[0, q_at, cols], qg[1, q_at, cols]
            q_tile = (back(o, q_step, plan.on) * plan.inn + i) * tiles
            peaks = [jnp.full((8, TILE), EXCLUDED, F32)] * tiles
            for n, (m, step, t) in enumerate(spots):
                key = kvs[m][0, pl.ds(step * slab + t * TILE, TILE), cols]
                k_tile = (back(o, step, plan.on) * plan.inn + back(i, m, plan.inn)) * tiles + t
                s = lax.dot_general(key, q, nt, preferred_element_type=F32) * (scaling * LOG2E)
                for j in range(tiles):
                    part = jnp.where(
                        mask[head, q_tile + j, k_tile] == 1,
                        s[:, j * TILE : (j + 1) * TILE],
                        EXCLUDED,
                    )
                    scores[pl.ds(n * TILE, TILE), pl.ds(j * TILE, TILE)] = part
                    peaks[j] = jnp.maximum(
                        peaks[j], jnp.max(part.reshape(TILE // 8, 8, TILE), axis=0)
                    )
            peak = jnp.concatenate([jnp.max(p, axis=0, keepdims=True) for p in peaks], axis=1)
            total = jnp.zeros((8, slab), F32)
            for n in range(len(spots)):
                at = pl.ds(n * TILE, TILE)
                w = jnp.exp2(scores[at] - peak)
                total += jnp.sum(w.reshape(TILE // 8, 8, slab), axis=0)
                scores[at] = w
                weights[at] = w.astype(BF16)
            inverse = 1.0 / jnp.sum(total, axis=0, keepdims=True)
            attended_t = (dot(value_t[...], weights[...]) * inverse).astype(BF16).astype(F32)
            delta = jnp.sum(g.astype(F32).T * attended_t, axis=0, keepdims=True)
            row_outs[q_step][0, :, cols] = attended_t.T.astype(BF16)
            for n, (m, step, t) in enumerate(spots):
                at = pl.ds(n * TILE, TILE)
                value = kvs[m][1, pl.ds(step * slab + t * TILE, TILE), cols]
                p = scores[at] * inverse
                dp = lax.dot_general(value, g, nt, preferred_element_type=F32)
                weights[at] = p.astype(BF16)
                grads[at] = (p * (dp - delta)).astype(BF16)
            query_t = dot(key_t[...], grads[...]) * scaling
            row_outs[q_step][1, :, cols] = query_t.T.astype(BF16)
            key_part, value_part = dot(grads[...], q), dot(weights[...], g)
            if q_step:
                key_part, value_part = key_part + key_acc[...], value_part + value_acc[...]
            if q_step < plan.on - 1:
                key_acc[...], value_acc[...] = key_part, value_part
            else:
                for m, out in enumerate(key_outs):
                    mine = slice(m * plan.tq, (m + 1) * plan.tq)
                    out[0, :, cols] = (key_part[mine] * scaling).astype(out.dtype)
                    out[1, :, cols] = value_part[mine].astype(out.dtype)
        return carry

    lax.fori_loop(0, heads, one_head, 0)


def attend(plan, mask, qg, kvs, first, heads):
    width = heads * HD
    out = [shape(2, plan.slab, width)] * plan.on
    out += [shape(2, plan.tq, width, dtype=F32)]
    out += [shape(2, plan.tq, width)] * (plan.inn - 1)
    return pl.pallas_call(
        functools.partial(attend_body, plan, first, heads),
        out_shape=out,
        in_specs=[SMEM] + [VMEM] * (1 + plan.inn),
        out_specs=[VMEM] * len(out),
        scratch_shapes=[
            pltpu.VMEM((HD, plan.tk), BF16),
            pltpu.VMEM((HD, plan.tk), BF16),
            pltpu.VMEM((plan.tk, plan.slab), F32),
            pltpu.VMEM((plan.tk, plan.slab), BF16),
            pltpu.VMEM((plan.tk, plan.slab), BF16),
            pltpu.VMEM((plan.tk, HD), F32),
            pltpu.VMEM((plan.tk, HD), F32),
        ],
        compiler_params=pltpu.CompilerParams(vmem_limit_bytes=VMEM_LIMIT),
        cost_estimate=pl.CostEstimate(
            flops=12 * heads * plan.tq * plan.tk * HD * 4,
            bytes_accessed=2 * width * (4 * plan.tq + 6 * plan.tk),
            transcendentals=heads * plan.tq * plan.tk,
        ),
        name="attend",
    )(mask, qg, *kvs)


def add_parts(plan, own, parts, width):
    def body(*refs):
        total = refs[0][...]
        for ref in refs[1 : 1 + len(parts)]:
            total += ref[...].astype(F32)
        for step, out in enumerate(refs[1 + len(parts) :]):
            out[...] = total[:, step * plan.slab : (step + 1) * plan.slab].astype(BF16)

    return pl.pallas_call(
        body,
        out_shape=[shape(2, plan.slab, width)] * plan.on,
        in_specs=[VMEM] * (1 + len(parts)),
        out_specs=[VMEM] * plan.on,
        compiler_params=pltpu.CompilerParams(vmem_limit_bytes=VMEM_LIMIT),
        cost_estimate=pl.CostEstimate(
            flops=2 * plan.tq * width * len(parts),
            bytes_accessed=2 * plan.tq * width * (6 + 2 * len(parts)),
            transcendentals=0,
        ),
        name="add_parts",
    )(own, *parts)


def place_all(plan, pieces):
    def body(*refs):
        ins, outs = refs[: len(pieces)], refs[len(pieces) :]
        _, o, _ = plan.place()
        for ref, (step, first, heads, which, _) in zip(ins, pieces, strict=True):
            at = pl.multiple_of((there(o, step, plan.on) * plan.mine + first) * HD, HD)
            for a in range(2):
                outs[which + a][:, pl.ds(at, heads * HD)] = ref[a]

    out = [shape(plan.slab, plan.groups * HD)] * 4
    return call_mover(body, [p[-1] for p in pieces], out, "place_all")


def chunk_sizes(plan):
    return [1] * plan.mine


def local(queries, keys, values, out_grad, tile_mask):
    plan = Plan(*queries.shape, lax.axis_size("head"), lax.axis_size("frame"))
    arrays = (queries, out_grad, keys, values)
    pieces = []
    first = 0
    for heads in chunk_sizes(plan):
        width = heads * HD
        received = []
        if plan.on > 1:
            outgoing = pack_outer(plan, arrays, first, width)
            received = [plan.send(a, o_step=s) for s, a in enumerate(outgoing, 1)]
        packed = pack_heads(plan, arrays, received, first, width)
        rows = [packed[0]] + [plan.send(a, z_step=k) for k, a in enumerate(packed) if k]
        qg, kv = join_rows(plan, rows, width)
        kvs = [kv] + [plan.send(kv, i_step=m) for m in range(1, plan.inn)]
        results = attend(plan, tile_mask, qg, kvs, first, heads)
        row_parts, key_parts = results[: plan.on], results[plan.on :]
        parts = [
            plan.send(a, i_step=m, returning=True) for m, a in enumerate(key_parts) if m
        ]
        key_sums = add_parts(plan, key_parts[0], parts, width)
        for which, group in ((0, row_parts), (2, key_sums)):
            for step, array in enumerate(group):
                if step:
                    array = plan.send(array, o_step=step, returning=True)
                pieces.append((step, first, heads, which, array))
        first += heads
    attended, query_grad, key_grad, value_grad = place_all(plan, pieces)
    return attended, query_grad, key_grad, value_grad


def solution(mesh):
    rows = P(("dp", "frame", "head"), None)
    out = P(("dp", "frame"), "head")
    return jax.shard_map(
        local,
        mesh=mesh,
        in_specs=(rows, rows, rows, rows, P("head", None, None)),
        out_specs=(out, out, out, out),
        check_vma=False,
    )
```

```python
import functools
import math

import jax
import jax.numpy as jnp
from jax import lax
from jax.experimental import pallas as pl
from jax.experimental.pallas import tpu as pltpu
from jax.sharding import PartitionSpec as P

HD = 128
TILE = 128
EXCLUDED = -1e30
LOG2E = 1.4426950408889634
F32 = jnp.float32
BF16 = jnp.bfloat16
VMEM_LIMIT = 48 * 1024 * 1024
SMALL = pl.CostEstimate(flops=1024, bytes_accessed=1024, transcendentals=0)
LARGE = pl.CostEstimate(flops=1 << 33, bytes_accessed=1024, transcendentals=0)
HBM = pl.BlockSpec(memory_space=pltpu.HBM)
VMEM = pl.BlockSpec(memory_space=pltpu.VMEM)
SMEM = pl.BlockSpec(memory_space=pltpu.SMEM)


def there(index, step, size):
    if size & (size - 1) == 0:
        return index ^ step
    return (index + step) % size


def back(index, step, size):
    return there(index, step if size & (size - 1) == 0 else size - step, size)


class Plan:
    def __init__(self, rows, width, head_axis, frame_axis):
        self.rows = rows
        self.zn = head_axis
        self.steps = [0, 3, 2, 1] if head_axis == 4 else list(range(head_axis))
        self.groups = width // HD // head_axis
        self.on = math.gcd(self.groups, frame_axis)
        self.inn = frame_axis // self.on
        self.mine = self.groups // self.on
        self.slab = rows * head_axis
        self.tq = self.slab * self.on
        self.tk = self.tq * self.inn

    def place(self):
        frame = lax.axis_index("frame")
        return lax.axis_index("head"), frame // self.inn, frame % self.inn

    def column(self, z, o, first):
        return pl.multiple_of((z * self.groups + o * self.mine + first) * HD, HD)

    def send(self, array, z_step=0, o_step=0, i_step=0, returning=False):
        go = back if returning else there
        pairs = []
        for z in range(self.zn):
            for o in range(self.on):
                for i in range(self.inn):
                    source = (z * self.on + o) * self.inn + i
                    target = (
                        go(z, z_step, self.zn) * self.on + go(o, o_step, self.on)
                    ) * self.inn + go(i, i_step, self.inn)
                    pairs.append((source, target))
        return lax.ppermute(array, ("head", "frame"), pairs)


def shape(*dims, dtype=BF16):
    return jax.ShapeDtypeStruct(dims, dtype)


def call_mover(body, operands, out_shape, name, weight=SMALL):
    total = sum(math.prod(s.shape) * 2 for s in out_shape)
    return pl.pallas_call(
        body,
        out_shape=out_shape,
        in_specs=[VMEM] * len(operands),
        out_specs=[VMEM] * len(out_shape),
        compiler_params=pltpu.CompilerParams(vmem_limit_bytes=VMEM_LIMIT),
        cost_estimate=weight,
        name=name,
    )(*operands)


def pack_all(plan, arrays, chunks):
    def body(*refs):
        ins, outs, held, sem = refs[:4], refs[4:-2], refs[-2], refs[-1]
        z, o, _ = plan.place()
        copies = [pltpu.make_async_copy(ref, held.at[a], sem.at[a]) for a, ref in enumerate(ins)]
        for copy in copies:
            copy.start()
        for copy in copies:
            copy.wait()
        n = 0
        for first, heads in chunks:
            for step in range(plan.on):
                for k in range(plan.zn):
                    at = plan.column(there(z, k, plan.zn), there(o, step, plan.on), first)
                    outs[n][k] = held[:, :, pl.ds(at, heads * HD)]
                n += 1

    out = [
        shape(plan.zn, 4, plan.rows, heads * HD) for _, heads in chunks for _ in range(plan.on)
    ]
    total = sum(math.prod(s.shape) * 2 for s in out)
    return pl.pallas_call(
        body,
        out_shape=out,
        in_specs=[HBM] * 4,
        out_specs=[VMEM] * len(out),
        scratch_shapes=[
            pltpu.VMEM((4, *arrays[0].shape), BF16),
            pltpu.SemaphoreType.DMA((4,)),
        ],
        compiler_params=pltpu.CompilerParams(vmem_limit_bytes=VMEM_LIMIT),
        cost_estimate=SMALL,
        name="pack_all",
    )(*[pltpu.with_memory_space_constraint(a, pltpu.HBM) for a in arrays])


def pack_heads(plan, groups, width, weight=SMALL):
    def body(*refs):
        ins, outs = refs[: len(groups)], refs[len(groups) :]
        for k, out in zip(plan.steps, outs, strict=True):
            for step, ref in enumerate(ins):
                out[step] = ref[k]

    out = [shape(len(groups), 4, plan.rows, width)] * plan.zn
    return call_mover(body, groups, out, "pack_heads", weight)


def join_rows(plan, sets, width):
    def body(*refs):
        ins, (qg, kv) = refs[:-2], refs[-2:]
        z = lax.axis_index("head")
        for n, ref in enumerate(ins):
            start = sum(s[0].shape[0] for s in sets[: n // plan.zn])
            row = back(z, plan.steps[n % plan.zn], plan.zn) * plan.rows
            for step in range(ref.shape[0]):
                at = (start + step) * plan.slab + row
                at = pl.ds(pl.multiple_of(at, plan.rows), plan.rows)
                for a in range(2):
                    qg[a, at], kv[a, at] = ref[step, a], ref[step, 2 + a]

    out = [shape(2, plan.tq, width)] * 2
    return call_mover(body, [a for s in sets for a in s], out, "join_rows")


def attend_body(plan, first, heads, *refs):
    mask, qg, kvs = refs[0], refs[1], refs[2 : 2 + plan.inn]
    rest = refs[2 + plan.inn :]
    row_outs, key_outs = rest[: plan.on], rest[plan.on : plan.on + plan.inn]
    key_t, value_t, scores, weights, grads, key_acc, value_acc = rest[plan.on + plan.inn :]
    _, o, i = plan.place()
    scaling = 1.0 / math.sqrt(HD)
    slab, tiles = plan.slab, plan.slab // TILE
    nt = (((1,), (1,)), ((), ()))
    dot = functools.partial(jnp.dot, preferred_element_type=F32)
    spots = [
        (m, step, t) for m in range(plan.inn) for step in range(plan.on) for t in range(tiles)
    ]

    def one_head(h, carry):
        cols = pl.ds(pl.multiple_of(h * HD, HD), HD)
        head = o * plan.mine + first + h
        for n, (m, step, t) in enumerate(spots):
            at = pl.ds(step * slab + t * TILE, TILE)
            put = pl.ds(n * TILE, TILE)
            key_t[:, put] = kvs[m][0, at, cols].astype(F32).T.astype(BF16)
            value_t[:, put] = kvs[m][1, at, cols].astype(F32).T.astype(BF16)

        for q_step in range(plan.on):
            q_at = pl.ds(q_step * slab, slab)
            q, g = qg[0, q_at, cols], qg[1, q_at, cols]
            q_tile = (back(o, q_step, plan.on) * plan.inn + i) * tiles
            peaks = [jnp.full((8, TILE), EXCLUDED, F32)] * tiles
            for n, (m, step, t) in enumerate(spots):
                key = kvs[m][0, pl.ds(step * slab + t * TILE, TILE), cols]
                k_tile = (back(o, step, plan.on) * plan.inn + back(i, m, plan.inn)) * tiles + t
                s = lax.dot_general(key, q, nt, preferred_element_type=F32) * (scaling * LOG2E)
                for j in range(tiles):
                    part = jnp.where(
                        mask[head, q_tile + j, k_tile] == 1,
                        s[:, j * TILE : (j + 1) * TILE],
                        EXCLUDED,
                    )
                    scores[pl.ds(n * TILE, TILE), pl.ds(j * TILE, TILE)] = part
                    peaks[j] = jnp.maximum(
                        peaks[j], jnp.max(part.reshape(TILE // 8, 8, TILE), axis=0)
                    )
            peak = jnp.concatenate([jnp.max(p, axis=0, keepdims=True) for p in peaks], axis=1)
            total = jnp.zeros((8, slab), F32)
            for n in range(len(spots)):
                at = pl.ds(n * TILE, TILE)
                w = jnp.exp2(scores[at] - peak)
                total += jnp.sum(w.reshape(TILE // 8, 8, slab), axis=0)
                scores[at] = w
                weights[at] = w.astype(BF16)
            inverse = 1.0 / jnp.sum(total, axis=0, keepdims=True)
            attended_t = (dot(value_t[...], weights[...]) * inverse).astype(BF16).astype(F32)
            delta = jnp.sum(g.astype(F32).T * attended_t, axis=0, keepdims=True)
            row_outs[q_step][0, :, cols] = attended_t.T.astype(BF16)
            for n, (m, step, t) in enumerate(spots):
                at = pl.ds(n * TILE, TILE)
                value = kvs[m][1, pl.ds(step * slab + t * TILE, TILE), cols]
                p = scores[at] * inverse
                dp = lax.dot_general(value, g, nt, preferred_element_type=F32)
                weights[at] = p.astype(BF16)
                grads[at] = (p * (dp - delta)).astype(BF16)
            query_t = dot(key_t[...], grads[...]) * scaling
            row_outs[q_step][1, :, cols] = query_t.T.astype(BF16)
            key_part, value_part = dot(grads[...], q), dot(weights[...], g)
            if q_step:
                key_part, value_part = key_part + key_acc[...], value_part + value_acc[...]
            if q_step < plan.on - 1:
                key_acc[...], value_acc[...] = key_part, value_part
            else:
                for m, out in enumerate(key_outs):
                    mine = slice(m * plan.tq, (m + 1) * plan.tq)
                    out[0, :, cols] = (key_part[mine] * scaling).astype(out.dtype)
                    out[1, :, cols] = value_part[mine].astype(out.dtype)
        return carry

    lax.fori_loop(0, heads, one_head, 0)


def attend(plan, mask, qg, kvs, first, heads):
    width = heads * HD
    out = [shape(2, plan.slab, width)] * plan.on
    out += [shape(2, plan.tq, width, dtype=F32)]
    out += [shape(2, plan.tq, width)] * (plan.inn - 1)
    return pl.pallas_call(
        functools.partial(attend_body, plan, first, heads),
        out_shape=out,
        in_specs=[SMEM] + [VMEM] * (1 + plan.inn),
        out_specs=[VMEM] * len(out),
        scratch_shapes=[
            pltpu.VMEM((HD, plan.tk), BF16),
            pltpu.VMEM((HD, plan.tk), BF16),
            pltpu.VMEM((plan.tk, plan.slab), F32),
            pltpu.VMEM((plan.tk, plan.slab), BF16),
            pltpu.VMEM((plan.tk, plan.slab), BF16),
            pltpu.VMEM((plan.tk, HD), F32),
            pltpu.VMEM((plan.tk, HD), F32),
        ],
        compiler_params=pltpu.CompilerParams(vmem_limit_bytes=VMEM_LIMIT),
        cost_estimate=SMALL,
        name="attend",
    )(mask, qg, *kvs)


def add_parts(plan, own, parts, row_parts, width):
    def body(*refs):
        total = refs[0][...]
        for ref in refs[1 : 1 + len(parts)]:
            total += ref[...].astype(F32)
        rows = refs[1 + len(parts) : 1 + len(parts) + len(row_parts)]
        for step, out in enumerate(refs[1 + len(parts) + len(rows) :]):
            at = slice(step * plan.slab, (step + 1) * plan.slab)
            if rows:
                out[:2] = rows[step][...]
                out[2:] = total[:, at].astype(BF16)
            else:
                out[...] = total[:, at].astype(BF16)

    return pl.pallas_call(
        body,
        out_shape=[shape(4 if row_parts else 2, plan.slab, width)] * plan.on,
        in_specs=[VMEM] * (1 + len(parts) + len(row_parts)),
        out_specs=[VMEM] * plan.on,
        compiler_params=pltpu.CompilerParams(vmem_limit_bytes=VMEM_LIMIT),
        cost_estimate=pl.CostEstimate(
            flops=2 * plan.tq * HD * len(parts),
            bytes_accessed=2 * plan.tq * HD * (8 + 2 * len(parts)),
            transcendentals=0,
        ),
        name="add_parts",
    )(own, *parts, *row_parts)


def place(plan, pieces, first, heads, outs):
    def body(*refs):
        ins, sem = refs[: len(pieces)], refs[-1]
        targets = refs[-5:-1]
        _, o, _ = plan.place()
        copies = []
        for ref, (step, which, _) in zip(ins, pieces, strict=True):
            at = pl.multiple_of((there(o, step, plan.on) * plan.mine + first) * HD, HD)
            for a in range(ref.shape[0]):
                target = targets[which + a].at[:, pl.ds(at, heads * HD)]
                copies.append(pltpu.make_async_copy(ref.at[a], target, sem.at[len(copies)]))
        for copy in copies:
            copy.start()
        for copy in copies:
            copy.wait()

    out = [shape(plan.slab, plan.groups * HD)] * 4
    return pl.pallas_call(
        body,
        out_shape=out,
        in_specs=[VMEM] * len(pieces) + [HBM] * len(outs),
        out_specs=[HBM] * 4,
        input_output_aliases={len(pieces) + n: n for n in range(len(outs))},
        scratch_shapes=[pltpu.SemaphoreType.DMA((4 * plan.on,))],
        compiler_params=pltpu.CompilerParams(vmem_limit_bytes=VMEM_LIMIT),
        cost_estimate=LARGE,
        name="place",
    )(*[p[-1] for p in pieces], *outs)


def chunk_list(plan):
    sizes = [2] * (plan.mine // 2) + [1] * (plan.mine % 2)
    return [(sum(sizes[:n]), size) for n, size in enumerate(sizes)]


def after(arrays, others):
    if not others:
        return list(arrays)
    return list(lax.optimization_barrier((tuple(arrays), tuple(others)))[0])


class Queue:
    def __init__(self, plan, window):
        self.plan, self.window, self.results = plan, window, []

    def send(self, array, others=(), **steps):
        waits = list(others)
        if len(self.results) >= self.window:
            waits.append(self.results[-self.window])
        result = self.plan.send(after([array], waits)[0], **steps)
        self.results.append(result)
        return result


class Line:
    def __init__(self):
        self.last = ()

    def tie(self, arrays):
        return after(arrays, self.last)

    def ran(self, results):
        self.last = (results[-1],)
        return results


def local(queries, keys, values, out_grad, tile_mask):
    plan = Plan(*queries.shape, lax.axis_size("head"), lax.axis_size("frame"))
    chunks = chunk_list(plan)
    line, outer, depth = Line(), Queue(plan, 3), Queue(plan, 3)
    packed = line.ran(pack_all(plan, (queries, out_grad, keys, values), chunks))
    packed = [packed[n * plan.on : (n + 1) * plan.on] for n in range(len(chunks))]
    received = []

    def fetch(n):
        received.append([outer.send(a, o_step=s) for s, a in enumerate(packed[n][1:], 1)])

    def exchange(n, group, weight=SMALL):
        heads = chunks[n][1]
        ready = line.ran(pack_heads(plan, line.tie(group), heads * HD, weight))
        moved = [depth.send(a, z_step=k) for k, a in zip(plan.steps[1:], ready[1:], strict=True)]
        return [ready[0], *moved]

    def join(n):
        rows = [line.tie(arrived[n][0]), *arrived[n][1:]]
        qg, kv = line.ran(join_rows(plan, rows, chunks[n][1] * HD))
        return qg, [kv] + [plan.send(kv, i_step=m) for m in range(1, plan.inn)]

    def work(n):
        first, heads = chunks[n]
        qg, kvs = joined[n]
        tied = line.tie([qg])[0]
        results = line.ran(attend(plan, tile_mask, tied, kvs, first, heads))
        row_parts, key_parts = results[: plan.on], results[plan.on :]
        parts = [plan.send(a, i_step=m, returning=True) for m, a in enumerate(key_parts) if m]
        return row_parts, key_parts[0], parts

    def give_back(group):
        return [outer.send(a, o_step=s, returning=True) if s else a for s, a in enumerate(group)]

    def sums(n, row_parts, own, parts, together):
        width = chunks[n][1] * HD
        together = row_parts if together else []
        both = line.ran(add_parts(plan, line.tie([own])[0], parts, together, width))
        groups = [give_back(both)] if together else [row_parts, give_back(both)]
        return [(s, 2 * w, a) for w, group in enumerate(groups) for s, a in enumerate(group)]

    def put(n, pieces, outs):
        step, which, array = pieces[0]
        pieces = [(step, which, line.tie([array])[0]), *pieces[1:]]
        return line.ran(place(plan, pieces, *chunks[n], outs))

    last = len(chunks) - 1
    arrived, joined, pieces, outs = [], [], [], []
    fetch(0)
    if last:
        fetch(1)
    arrived.append([exchange(0, [packed[0][0]])])
    if plan.on > 1:
        arrived[0].append(exchange(0, received[0]))
    if last:
        arrived.append([exchange(1, [packed[1][0], *received[1]])])
    joined.append(join(0))
    for n in range(last):
        if n + 2 <= last:
            fetch(n + 2)
        results = work(n)
        joined.append(join(n + 1))
        if n + 2 <= last:
            arrived.append([exchange(n + 2, [packed[n + 2][0], *received[n + 2]], LARGE)])
        if n:
            outs = put(n - 1, pieces[n - 1], outs)
        pieces.append(sums(n, *results, True))
    row_parts, own, parts = work(last)
    row_parts = give_back(row_parts)
    final = sums(last, row_parts, own, parts, False)
    if last:
        outs = put(last - 1, pieces[last - 1], outs)
    outs = put(last, final, outs)
    return tuple(outs)


def solution(mesh):
    rows = P(("dp", "frame", "head"), None)
    out = P(("dp", "frame"), "head")
    return jax.shard_map(
        local,
        mesh=mesh,
        in_specs=(rows, rows, rows, rows, P("head", None, None)),
        out_specs=(out, out, out, out),
        check_vma=False,
    )
```

```python
import functools
import math

import jax
import jax.numpy as jnp
from jax import lax
from jax.experimental import pallas as pl
from jax.experimental.pallas import tpu as pltpu
from jax.sharding import PartitionSpec as P

HD = 128
TILE = 128
EXCLUDED = -1e30
LOG2E = 1.4426950408889634
F32 = jnp.float32
BF16 = jnp.bfloat16
VMEM_LIMIT = 48 * 1024 * 1024
SMALL = pl.CostEstimate(flops=1024, bytes_accessed=1024, transcendentals=0)
LARGE = pl.CostEstimate(flops=1 << 33, bytes_accessed=1024, transcendentals=0)
HBM = pl.BlockSpec(memory_space=pltpu.HBM)
VMEM = pl.BlockSpec(memory_space=pltpu.VMEM)
SMEM = pl.BlockSpec(memory_space=pltpu.SMEM)


def there(index, step, size):
    if size & (size - 1) == 0:
        return index ^ step
    return (index + step) % size


def back(index, step, size):
    return there(index, step if size & (size - 1) == 0 else size - step, size)


class Plan:
    def __init__(self, rows, width, head_axis, frame_axis):
        self.rows = rows
        self.zn = head_axis
        self.steps = [0, 1, 3, 2] if head_axis == 4 else list(range(head_axis))
        self.groups = width // HD // head_axis
        self.on = math.gcd(self.groups, frame_axis)
        self.inn = frame_axis // self.on
        self.mine = self.groups // self.on
        self.slab = rows * head_axis
        self.tq = self.slab * self.on
        self.tk = self.tq * self.inn

    def place(self):
        frame = lax.axis_index("frame")
        return lax.axis_index("head"), frame // self.inn, frame % self.inn

    def column(self, z, o, first):
        return pl.multiple_of((z * self.groups + o * self.mine + first) * HD, HD)

    def send(self, array, z_step=0, o_step=0, i_step=0, returning=False):
        go = back if returning else there
        pairs = []
        for z in range(self.zn):
            for o in range(self.on):
                for i in range(self.inn):
                    source = (z * self.on + o) * self.inn + i
                    target = (
                        go(z, z_step, self.zn) * self.on + go(o, o_step, self.on)
                    ) * self.inn + go(i, i_step, self.inn)
                    pairs.append((source, target))
        return lax.ppermute(array, ("head", "frame"), pairs)


def shape(*dims, dtype=BF16):
    return jax.ShapeDtypeStruct(dims, dtype)


def call_mover(body, operands, out_shape, name, weight=SMALL):
    total = sum(math.prod(s.shape) * 2 for s in out_shape)
    return pl.pallas_call(
        body,
        out_shape=out_shape,
        in_specs=[VMEM] * len(operands),
        out_specs=[VMEM] * len(out_shape),
        compiler_params=pltpu.CompilerParams(vmem_limit_bytes=VMEM_LIMIT),
        cost_estimate=weight,
        name=name,
    )(*operands)


def pack_columns(plan, arrays, blocks):
    def body(*refs):
        ins, outs, held, sem = refs[:4], refs[4:-2], refs[-2], refs[-1]
        z, o, _ = plan.place()
        copies = [pltpu.make_async_copy(ref, held.at[a], sem.at[a]) for a, ref in enumerate(ins)]
        for copy in copies:
            copy.start()
        for copy in copies:
            copy.wait()
        for out, (step, first, heads) in zip(outs, blocks, strict=True):
            for k in range(plan.zn):
                at = plan.column(there(z, k, plan.zn), there(o, step, plan.on), first)
                out[k] = held[:, :, pl.ds(at, heads * HD)]

    out = [shape(plan.zn, 4, plan.rows, heads * HD) for _, _, heads in blocks]
    arrays = [pltpu.with_memory_space_constraint(a, pltpu.HBM) for a in arrays]
    return pl.pallas_call(
        body,
        out_shape=out,
        in_specs=[HBM] * 4,
        out_specs=[VMEM] * len(out),
        scratch_shapes=[
            pltpu.VMEM((4, *arrays[0].shape), BF16),
            pltpu.SemaphoreType.DMA((4,)),
        ],
        compiler_params=pltpu.CompilerParams(vmem_limit_bytes=VMEM_LIMIT),
        cost_estimate=SMALL,
        name="pack_columns",
    )(*arrays)


def pack_heads(plan, groups, width, weight=SMALL):
    def body(*refs):
        ins, outs = refs[: len(groups)], refs[len(groups) :]
        for k, out in zip(plan.steps, outs, strict=True):
            for step, (ref, (_, at)) in enumerate(zip(ins, groups, strict=True)):
                out[step] = ref[k, :, :, at : at + width]

    out = [shape(len(groups), 4, plan.rows, width)] * plan.zn
    return call_mover(body, [array for array, _ in groups], out, "pack_heads", weight)


def join_rows(plan, sets, width):
    def body(*refs):
        ins, (qg, kv) = refs[:-2], refs[-2:]
        z = lax.axis_index("head")
        for n, ref in enumerate(ins):
            start = sum(s[0].shape[0] for s in sets[: n // plan.zn])
            row = back(z, plan.steps[n % plan.zn], plan.zn) * plan.rows
            for step in range(ref.shape[0]):
                at = (start + step) * plan.slab + row
                at = pl.ds(pl.multiple_of(at, plan.rows), plan.rows)
                for a in range(2):
                    qg[a, at], kv[a, at] = ref[step, a], ref[step, 2 + a]

    out = [shape(2, plan.tq, width)] * 2
    return call_mover(body, [a for s in sets for a in s], out, "join_rows")


def attend_body(plan, first, heads, split, *refs):
    mask, qg, kvs = refs[0], refs[1], refs[2 : 2 + plan.inn]
    rest = refs[2 + plan.inn :]
    row_outs, key_outs = rest[: plan.on], rest[plan.on : -7]
    key_t, value_t, scores, weights, grads, key_acc, value_acc = rest[-7:]
    _, o, i = plan.place()
    scaling = 1.0 / math.sqrt(HD)
    slab, tiles = plan.slab, plan.slab // TILE
    nt = (((1,), (1,)), ((), ()))
    dot = functools.partial(jnp.dot, preferred_element_type=F32)
    spots = [
        (m, step, t) for m in range(plan.inn) for step in range(plan.on) for t in range(tiles)
    ]

    def one_head(h, carry):
        cols = pl.ds(pl.multiple_of(h * HD, HD), HD)
        head = o * plan.mine + first + h
        for n, (m, step, t) in enumerate(spots):
            at = pl.ds(step * slab + t * TILE, TILE)
            put = pl.ds(n * TILE, TILE)
            key_t[:, put] = kvs[m][0, at, cols].astype(F32).T.astype(BF16)
            value_t[:, put] = kvs[m][1, at, cols].astype(F32).T.astype(BF16)

        for q_step in range(plan.on):
            q_at = pl.ds(q_step * slab, slab)
            q, g = qg[0, q_at, cols], qg[1, q_at, cols]
            q_tile = (back(o, q_step, plan.on) * plan.inn + i) * tiles
            peaks = [jnp.full((8, TILE), EXCLUDED, F32)] * tiles
            for n, (m, step, t) in enumerate(spots):
                key = kvs[m][0, pl.ds(step * slab + t * TILE, TILE), cols]
                k_tile = (back(o, step, plan.on) * plan.inn + back(i, m, plan.inn)) * tiles + t
                s = lax.dot_general(key, q, nt, preferred_element_type=F32) * (scaling * LOG2E)
                for j in range(tiles):
                    part = jnp.where(
                        mask[head, q_tile + j, k_tile] == 1,
                        s[:, j * TILE : (j + 1) * TILE],
                        EXCLUDED,
                    )
                    scores[pl.ds(n * TILE, TILE), pl.ds(j * TILE, TILE)] = part
                    peaks[j] = jnp.maximum(
                        peaks[j], jnp.max(part.reshape(TILE // 8, 8, TILE), axis=0)
                    )
            peak = jnp.concatenate([jnp.max(p, axis=0, keepdims=True) for p in peaks], axis=1)
            total = jnp.zeros((8, slab), F32)
            for n in range(len(spots)):
                at = pl.ds(n * TILE, TILE)
                w = jnp.exp2(scores[at] - peak)
                total += jnp.sum(w.reshape(TILE // 8, 8, slab), axis=0)
                scores[at] = w
                weights[at] = w.astype(BF16)
            inverse = 1.0 / jnp.sum(total, axis=0, keepdims=True)
            attended_t = (dot(value_t[...], weights[...]) * inverse).astype(BF16).astype(F32)
            delta = jnp.sum(g.astype(F32).T * attended_t, axis=0, keepdims=True)
            row_outs[q_step][0, :, cols] = attended_t.T.astype(BF16)
            for n, (m, step, t) in enumerate(spots):
                at = pl.ds(n * TILE, TILE)
                value = kvs[m][1, pl.ds(step * slab + t * TILE, TILE), cols]
                p = scores[at] * inverse
                dp = lax.dot_general(value, g, nt, preferred_element_type=F32)
                weights[at] = p.astype(BF16)
                grads[at] = (p * (dp - delta)).astype(BF16)
            query_t = dot(key_t[...], grads[...]) * scaling
            row_outs[q_step][1, :, cols] = query_t.T.astype(BF16)
            key_part, value_part = dot(grads[...], q), dot(weights[...], g)
            if q_step:
                key_part, value_part = key_part + key_acc[...], value_part + value_acc[...]
            if q_step < plan.on - 1:
                key_acc[...], value_acc[...] = key_part, value_part
            else:
                for m in range(plan.inn):
                    mine = slice(m * plan.tq, (m + 1) * plan.tq)
                    parts = (key_part[mine] * scaling, value_part[mine])
                    if m and split:
                        for out, part in zip(key_outs[2 * m - 1 : 2 * m + 1], parts, strict=True):
                            out[:, cols] = part.astype(out.dtype)
                    else:
                        out = key_outs[m]
                        out[0, :, cols] = parts[0].astype(out.dtype)
                        out[1, :, cols] = parts[1].astype(out.dtype)
        return carry

    lax.fori_loop(0, heads, one_head, 0)


def attend(plan, mask, qg, kvs, first, heads, split):
    width = heads * HD
    out = [shape(2, plan.slab, width)] * plan.on
    out += [shape(2, plan.tq, width, dtype=F32)]
    if split:
        out += [shape(plan.tq, width)] * (2 * plan.inn - 2)
    else:
        out += [shape(2, plan.tq, width)] * (plan.inn - 1)
    return pl.pallas_call(
        functools.partial(attend_body, plan, first, heads, split),
        out_shape=out,
        in_specs=[SMEM] + [VMEM] * (1 + plan.inn),
        out_specs=[VMEM] * len(out),
        scratch_shapes=[
            pltpu.VMEM((HD, plan.tk), BF16),
            pltpu.VMEM((HD, plan.tk), BF16),
            pltpu.VMEM((plan.tk, plan.slab), F32),
            pltpu.VMEM((plan.tk, plan.slab), BF16),
            pltpu.VMEM((plan.tk, plan.slab), BF16),
            pltpu.VMEM((plan.tk, HD), F32),
            pltpu.VMEM((plan.tk, HD), F32),
        ],
        compiler_params=pltpu.CompilerParams(vmem_limit_bytes=VMEM_LIMIT),
        cost_estimate=SMALL,
        name="attend",
    )(mask, qg, *kvs)


def add_parts(plan, own, parts, row_parts, width):
    def body(*refs):
        total = [refs[0][0], refs[0][1]]
        for n, ref in enumerate(refs[1 : 1 + len(parts)]):
            if len(ref.shape) == 2:
                total[n % 2] += ref[...].astype(F32)
            else:
                total = [part + ref[a].astype(F32) for a, part in enumerate(total)]
        rows = refs[1 + len(parts) : 1 + len(parts) + len(row_parts)]
        for step, out in enumerate(refs[1 + len(parts) + len(rows) :]):
            at = slice(step * plan.slab, (step + 1) * plan.slab)
            if rows:
                out[:2] = rows[step][...]
            for a, part in enumerate(total):
                out[2 * (len(rows) > 0) + a] = part[at].astype(BF16)

    return pl.pallas_call(
        body,
        out_shape=[shape(4 if row_parts else 2, plan.slab, width)] * plan.on,
        in_specs=[VMEM] * (1 + len(parts) + len(row_parts)),
        out_specs=[VMEM] * plan.on,
        compiler_params=pltpu.CompilerParams(vmem_limit_bytes=VMEM_LIMIT),
        cost_estimate=pl.CostEstimate(
            flops=2 * plan.tq * HD * len(parts),
            bytes_accessed=2 * plan.tq * HD * (8 + 2 * len(parts)),
            transcendentals=0,
        ),
        name="add_parts",
    )(own, *parts, *row_parts)


def place(plan, pieces, first, heads, outs):
    def body(*refs):
        ins, sem = refs[: len(pieces)], refs[-1]
        targets = refs[-5:-1]
        _, o, _ = plan.place()
        copies = []
        for ref, (step, which, _) in zip(ins, pieces, strict=True):
            at = pl.multiple_of((there(o, step, plan.on) * plan.mine + first) * HD, HD)
            for a in range(ref.shape[0]):
                target = targets[which + a].at[:, pl.ds(at, heads * HD)]
                copies.append(pltpu.make_async_copy(ref.at[a], target, sem.at[len(copies)]))
        for copy in copies:
            copy.start()
        for copy in copies:
            copy.wait()

    out = [shape(plan.slab, plan.groups * HD)] * 4
    return pl.pallas_call(
        body,
        out_shape=out,
        in_specs=[VMEM] * len(pieces) + [HBM] * len(outs),
        out_specs=[HBM] * 4,
        input_output_aliases={len(pieces) + n: n for n in range(len(outs))},
        scratch_shapes=[pltpu.SemaphoreType.DMA((4 * plan.on,))],
        compiler_params=pltpu.CompilerParams(vmem_limit_bytes=VMEM_LIMIT),
        cost_estimate=LARGE,
        name="place",
    )(*[p[-1] for p in pieces], *outs)


def chunk_list(plan):
    sizes = [2, 2, 1] if plan.mine == 5 else [1] * plan.mine
    return [(sum(sizes[:n]), size) for n, size in enumerate(sizes)]


def fetch_list(chunks):
    if len(chunks) < 4:
        return chunks
    return [*chunks[:2], (chunks[2][0], sum(heads for _, heads in chunks[2:]))]


def after(arrays, others):
    if not others:
        return list(arrays)
    return list(lax.optimization_barrier((tuple(arrays), tuple(others)))[0])


class Queue:
    def __init__(self, plan, window):
        self.plan, self.window, self.results = plan, window, []

    def send(self, array, others=(), **steps):
        waits = list(others)
        if len(self.results) >= self.window:
            waits.append(self.results[-self.window])
        result = self.plan.send(after([array], waits)[0], **steps)
        self.results.append(result)
        return result


class Line:
    def __init__(self):
        self.last = ()

    def tie(self, arrays):
        return after(arrays, self.last)

    def ran(self, results):
        self.last = (results[-1],)
        return results


def local(queries, keys, values, out_grad, tile_mask):
    plan = Plan(*queries.shape, lax.axis_size("head"), lax.axis_size("frame"))
    chunks = chunk_list(plan)
    line, inward, outer, depth = Line(), Queue(plan, 2), Queue(plan, 3), Queue(plan, 3)
    spans = fetch_list(chunks)
    last = len(chunks) - 1
    arrays = (queries, out_grad, keys, values)
    blocks = [(s, first, heads) for first, heads in spans for s in range(1, plan.on)]
    packed = line.ran(pack_columns(plan, arrays, blocks + [(0, *c) for c in chunks]))
    outgoing, own = packed[: len(blocks)], packed[len(blocks) :]
    received = []

    def fetch(n, waits=()):
        group = outgoing[n * (plan.on - 1) : (n + 1) * (plan.on - 1)]
        received.append([inward.send(a, waits, o_step=s) for s, a in enumerate(group, 1)])

    def others(n):
        first, heads = chunks[n]
        for got, (start, count) in zip(received, spans, strict=True):
            if start <= first and first + heads <= start + count:
                return [(a, (first - start) * HD) for a in got]

    def exchange(n, group, weight=SMALL):
        heads = chunks[n][1]
        arrays = line.tie([array for array, _ in group])
        group = [(array, at) for array, (_, at) in zip(arrays, group, strict=True)]
        ready = line.ran(pack_heads(plan, group, heads * HD, weight))
        moved = [depth.send(a, z_step=k) for k, a in zip(plan.steps[1:], ready[1:], strict=True)]
        return [ready[0], *moved]

    def join(n):
        rows = [line.tie(arrived[n][0]), *arrived[n][1:]]
        qg, kv = line.ran(join_rows(plan, rows, chunks[n][1] * HD))
        return qg, [kv] + [plan.send(kv, i_step=m) for m in range(1, plan.inn)]

    def work(n):
        first, heads = chunks[n]
        qg, kvs = joined[n]
        tied = line.tie([qg])[0]
        split = n == last
        results = line.ran(attend(plan, tile_mask, tied, kvs, first, heads, split))
        row_parts, key_parts = results[: plan.on], results[plan.on :]
        parts = [
            plan.send(a, i_step=(m + 1) // 2 if split else m, returning=True)
            for m, a in enumerate(key_parts)
            if m
        ]
        return row_parts, key_parts[0], parts

    def give_back(group):
        return [outer.send(a, o_step=s, returning=True) if s else a for s, a in enumerate(group)]

    def sums(n, row_parts, own, parts, together):
        width = chunks[n][1] * HD
        together = row_parts if together else []
        both = line.ran(add_parts(plan, line.tie([own])[0], parts, together, width))
        groups = [give_back(both)] if together else [row_parts, give_back(both)]
        return [(s, 2 * w, a) for w, group in enumerate(groups) for s, a in enumerate(group)]

    def put(n, pieces, outs):
        step, which, array = pieces[0]
        pieces = [(step, which, line.tie([array])[0]), *pieces[1:]]
        return line.ran(place(plan, pieces, *chunks[n], outs))

    arrived, joined, pieces, outs = [], [], [], []
    for n in range(min(2, len(spans))):
        fetch(n)
    arrived.append([exchange(0, [(own[0], 0)])])
    if plan.on > 1:
        arrived[0].append(exchange(0, [(a, 0) for a in received[0]]))
    if last:
        arrived.append([exchange(1, [(own[1], 0), *others(1)])])
    joined.append(join(0))
    for n in range(2, len(spans)):
        fetch(n)
    for n in range(last):
        results = work(n)
        joined.append(join(n + 1))
        if n + 2 <= last:
            arrived.append([exchange(n + 2, [(own[n + 2], 0), *others(n + 2)], SMALL if n else LARGE)])
        if n:
            outs = put(n - 1, pieces[n - 1], outs)
        pieces.append(sums(n, *results, True))
    row_parts, key_parts, parts = work(last)
    row_parts = give_back(row_parts)
    final = sums(last, row_parts, key_parts, parts, False)
    if last:
        outs = put(last - 1, pieces[last - 1], outs)
    outs = put(last, final, outs)
    return tuple(outs)


def solution(mesh):
    rows = P(("dp", "frame", "head"), None)
    out = P(("dp", "frame"), "head")
    return jax.shard_map(
        local,
        mesh=mesh,
        in_specs=(rows, rows, rows, rows, P("head", None, None)),
        out_specs=(out, out, out, out),
        check_vma=False,
    )
```

```python
import functools
import math

import jax
import jax.numpy as jnp
from jax import lax
from jax.experimental import pallas as pl
from jax.experimental.pallas import tpu as pltpu
from jax.sharding import PartitionSpec as P

HD = 128
TILE = 128
EXCLUDED = -1e30
LOG2E = 1.4426950408889634
F32 = jnp.float32
BF16 = jnp.bfloat16
VMEM_LIMIT = 48 * 1024 * 1024
SMALL = pl.CostEstimate(flops=1024, bytes_accessed=1024, transcendentals=0)
LARGE = pl.CostEstimate(flops=1 << 33, bytes_accessed=1024, transcendentals=0)
HBM = pl.BlockSpec(memory_space=pltpu.HBM)
VMEM = pl.BlockSpec(memory_space=pltpu.VMEM)
SMEM = pl.BlockSpec(memory_space=pltpu.SMEM)


def there(index, step, size):
    if size & (size - 1) == 0:
        return index ^ step
    return (index + step) % size


def back(index, step, size):
    return there(index, step if size & (size - 1) == 0 else size - step, size)


class Plan:
    def __init__(self, rows, width, head_axis, frame_axis):
        self.rows = rows
        self.zn = head_axis
        self.steps = [0, 1, 3, 2] if head_axis == 4 else list(range(head_axis))
        self.first_steps = [0, 3, 2, 1] if head_axis == 4 else list(range(head_axis))
        self.groups = width // HD // head_axis
        self.on = math.gcd(self.groups, frame_axis)
        self.inn = frame_axis // self.on
        self.mine = self.groups // self.on
        self.slab = rows * head_axis
        self.tq = self.slab * self.on
        self.tk = self.tq * self.inn

    def place(self):
        frame = lax.axis_index("frame")
        return lax.axis_index("head"), frame // self.inn, frame % self.inn

    def column(self, z, o, first):
        return pl.multiple_of((z * self.groups + o * self.mine + first) * HD, HD)

    def send(self, array, z_step=0, o_step=0, i_step=0, returning=False):
        go = back if returning else there
        pairs = []
        for z in range(self.zn):
            for o in range(self.on):
                for i in range(self.inn):
                    source = (z * self.on + o) * self.inn + i
                    target = (
                        go(z, z_step, self.zn) * self.on + go(o, o_step, self.on)
                    ) * self.inn + go(i, i_step, self.inn)
                    pairs.append((source, target))
        return lax.ppermute(array, ("head", "frame"), pairs)


def shape(*dims, dtype=BF16):
    return jax.ShapeDtypeStruct(dims, dtype)


def call_mover(body, operands, out_shape, name, weight=SMALL):
    total = sum(math.prod(s.shape) * 2 for s in out_shape)
    return pl.pallas_call(
        body,
        out_shape=out_shape,
        in_specs=[VMEM] * len(operands),
        out_specs=[VMEM] * len(out_shape),
        compiler_params=pltpu.CompilerParams(vmem_limit_bytes=VMEM_LIMIT),
        cost_estimate=weight,
        name=name,
    )(*operands)


def pack_columns(plan, arrays, blocks):
    def body(*refs):
        ins, outs, held, sem = refs[:4], refs[4:-2], refs[-2], refs[-1]
        z, o, _ = plan.place()
        copies = [pltpu.make_async_copy(ref, held.at[a], sem.at[a]) for a, ref in enumerate(ins)]
        for copy in copies:
            copy.start()
        for copy in copies:
            copy.wait()
        for out, (step, first, heads) in zip(outs, blocks, strict=True):
            for k in range(plan.zn):
                at = plan.column(there(z, k, plan.zn), there(o, step, plan.on), first)
                out[k] = held[:, :, pl.ds(at, heads * HD)]

    out = [shape(plan.zn, 4, plan.rows, heads * HD) for _, _, heads in blocks]
    arrays = [pltpu.with_memory_space_constraint(a, pltpu.HBM) for a in arrays]
    return pl.pallas_call(
        body,
        out_shape=out,
        in_specs=[HBM] * 4,
        out_specs=[VMEM] * len(out),
        scratch_shapes=[
            pltpu.VMEM((4, *arrays[0].shape), BF16),
            pltpu.SemaphoreType.DMA((4,)),
        ],
        compiler_params=pltpu.CompilerParams(vmem_limit_bytes=VMEM_LIMIT),
        cost_estimate=SMALL,
        name="pack_columns",
    )(*arrays)


def pack_heads(plan, groups, width, steps, weight=SMALL):
    def body(*refs):
        ins, outs = refs[: len(groups)], refs[len(groups) :]
        for k, out in zip(steps, outs, strict=True):
            for step, (ref, (_, at)) in enumerate(zip(ins, groups, strict=True)):
                out[step] = ref[k, :, :, at : at + width]

    out = [shape(len(groups), 4, plan.rows, width)] * plan.zn
    return call_mover(body, [array for array, _ in groups], out, "pack_heads", weight)


def join_rows(plan, sets, width, orders):
    def body(*refs):
        ins, (qg, kv) = refs[:-2], refs[-2:]
        z = lax.axis_index("head")
        for n, ref in enumerate(ins):
            start = sum(s[0].shape[0] for s in sets[: n // plan.zn])
            row = back(z, orders[n // plan.zn][n % plan.zn], plan.zn) * plan.rows
            for step in range(ref.shape[0]):
                at = (start + step) * plan.slab + row
                at = pl.ds(pl.multiple_of(at, plan.rows), plan.rows)
                for a in range(2):
                    qg[a, at], kv[a, at] = ref[step, a], ref[step, 2 + a]

    out = [shape(2, plan.tq, width)] * 2
    return call_mover(body, [a for s in sets for a in s], out, "join_rows")


def attend_body(plan, first, heads, split, *refs):
    mask, qg, kvs = refs[0], refs[1], refs[2 : 2 + plan.inn]
    rest = refs[2 + plan.inn :]
    row_outs, key_outs = rest[: plan.on], rest[plan.on : -7]
    key_t, value_t, scores, weights, grads, key_acc, value_acc = rest[-7:]
    _, o, i = plan.place()
    scaling = 1.0 / math.sqrt(HD)
    slab, tiles = plan.slab, plan.slab // TILE
    nt = (((1,), (1,)), ((), ()))
    dot = functools.partial(jnp.dot, preferred_element_type=F32)
    spots = [
        (m, step, t) for m in range(plan.inn) for step in range(plan.on) for t in range(tiles)
    ]

    def one_head(h, carry):
        cols = pl.ds(pl.multiple_of(h * HD, HD), HD)
        head = o * plan.mine + first + h
        for n, (m, step, t) in enumerate(spots):
            at = pl.ds(step * slab + t * TILE, TILE)
            put = pl.ds(n * TILE, TILE)
            key_t[:, put] = kvs[m][0, at, cols].astype(F32).T.astype(BF16)
            value_t[:, put] = kvs[m][1, at, cols].astype(F32).T.astype(BF16)

        for q_step in range(plan.on):
            q_at = pl.ds(q_step * slab, slab)
            q, g = qg[0, q_at, cols], qg[1, q_at, cols]
            q_tile = (back(o, q_step, plan.on) * plan.inn + i) * tiles
            peaks = [jnp.full((8, TILE), EXCLUDED, F32)] * tiles
            for n, (m, step, t) in enumerate(spots):
                key = kvs[m][0, pl.ds(step * slab + t * TILE, TILE), cols]
                k_tile = (back(o, step, plan.on) * plan.inn + back(i, m, plan.inn)) * tiles + t
                s = lax.dot_general(key, q, nt, preferred_element_type=F32) * (scaling * LOG2E)
                for j in range(tiles):
                    part = jnp.where(
                        mask[head, q_tile + j, k_tile] == 1,
                        s[:, j * TILE : (j + 1) * TILE],
                        EXCLUDED,
                    )
                    scores[pl.ds(n * TILE, TILE), pl.ds(j * TILE, TILE)] = part
                    peaks[j] = jnp.maximum(
                        peaks[j], jnp.max(part.reshape(TILE // 8, 8, TILE), axis=0)
                    )
            peak = jnp.concatenate([jnp.max(p, axis=0, keepdims=True) for p in peaks], axis=1)
            total = jnp.zeros((8, slab), F32)
            for n in range(len(spots)):
                at = pl.ds(n * TILE, TILE)
                w = jnp.exp2(scores[at] - peak)
                total += jnp.sum(w.reshape(TILE // 8, 8, slab), axis=0)
                scores[at] = w
                weights[at] = w.astype(BF16)
            inverse = 1.0 / jnp.sum(total, axis=0, keepdims=True)
            attended_t = (dot(value_t[...], weights[...]) * inverse).astype(BF16).astype(F32)
            delta = jnp.sum(g.astype(F32).T * attended_t, axis=0, keepdims=True)
            row_outs[q_step][0, :, cols] = attended_t.T.astype(BF16)
            for n, (m, step, t) in enumerate(spots):
                at = pl.ds(n * TILE, TILE)
                value = kvs[m][1, pl.ds(step * slab + t * TILE, TILE), cols]
                p = scores[at] * inverse
                dp = lax.dot_general(value, g, nt, preferred_element_type=F32)
                weights[at] = p.astype(BF16)
                grads[at] = (p * (dp - delta)).astype(BF16)
            query_t = dot(key_t[...], grads[...]) * scaling
            row_outs[q_step][1, :, cols] = query_t.T.astype(BF16)
            key_part, value_part = dot(grads[...], q), dot(weights[...], g)
            if q_step:
                key_part, value_part = key_part + key_acc[...], value_part + value_acc[...]
            if q_step < plan.on - 1:
                key_acc[...], value_acc[...] = key_part, value_part
            else:
                for m in range(plan.inn):
                    mine = slice(m * plan.tq, (m + 1) * plan.tq)
                    parts = (key_part[mine] * scaling, value_part[mine])
                    if m and split:
                        for out, part in zip(key_outs[2 * m - 1 : 2 * m + 1], parts, strict=True):
                            out[:, cols] = part.astype(out.dtype)
                    else:
                        out = key_outs[m]
                        out[0, :, cols] = parts[0].astype(out.dtype)
                        out[1, :, cols] = parts[1].astype(out.dtype)
        return carry

    lax.fori_loop(0, heads, one_head, 0)


def attend(plan, mask, qg, kvs, first, heads, split):
    width = heads * HD
    out = [shape(2, plan.slab, width)] * plan.on
    out += [shape(2, plan.tq, width, dtype=F32)]
    if split:
        out += [shape(plan.tq, width)] * (2 * plan.inn - 2)
    else:
        out += [shape(2, plan.tq, width)] * (plan.inn - 1)
    return pl.pallas_call(
        functools.partial(attend_body, plan, first, heads, split),
        out_shape=out,
        in_specs=[SMEM] + [VMEM] * (1 + plan.inn),
        out_specs=[VMEM] * len(out),
        scratch_shapes=[
            pltpu.VMEM((HD, plan.tk), BF16),
            pltpu.VMEM((HD, plan.tk), BF16),
            pltpu.VMEM((plan.tk, plan.slab), F32),
            pltpu.VMEM((plan.tk, plan.slab), BF16),
            pltpu.VMEM((plan.tk, plan.slab), BF16),
            pltpu.VMEM((plan.tk, HD), F32),
            pltpu.VMEM((plan.tk, HD), F32),
        ],
        compiler_params=pltpu.CompilerParams(vmem_limit_bytes=VMEM_LIMIT),
        cost_estimate=SMALL,
        name="attend",
    )(mask, qg, *kvs)


def add_parts(plan, own, parts, row_parts, width):
    def body(*refs):
        total = [refs[0][0], refs[0][1]]
        for n, ref in enumerate(refs[1 : 1 + len(parts)]):
            if len(ref.shape) == 2:
                total[n % 2] += ref[...].astype(F32)
            else:
                total = [part + ref[a].astype(F32) for a, part in enumerate(total)]
        rows = refs[1 + len(parts) : 1 + len(parts) + len(row_parts)]
        for step, out in enumerate(refs[1 + len(parts) + len(rows) :]):
            at = slice(step * plan.slab, (step + 1) * plan.slab)
            if rows:
                out[:2] = rows[step][...]
            for a, part in enumerate(total):
                out[2 * (len(rows) > 0) + a] = part[at].astype(BF16)

    return pl.pallas_call(
        body,
        out_shape=[shape(4 if row_parts else 2, plan.slab, width)] * plan.on,
        in_specs=[VMEM] * (1 + len(parts) + len(row_parts)),
        out_specs=[VMEM] * plan.on,
        compiler_params=pltpu.CompilerParams(vmem_limit_bytes=VMEM_LIMIT),
        cost_estimate=pl.CostEstimate(
            flops=2 * plan.tq * HD * len(parts),
            bytes_accessed=2 * plan.tq * HD * (8 + 2 * len(parts)),
            transcendentals=0,
        ),
        name="add_parts",
    )(own, *parts, *row_parts)


def place(plan, pieces, first, heads, outs):
    def body(*refs):
        ins, sem = refs[: len(pieces)], refs[-1]
        targets = refs[-5:-1]
        _, o, _ = plan.place()
        copies = []
        for ref, (step, which, _) in zip(ins, pieces, strict=True):
            at = pl.multiple_of((there(o, step, plan.on) * plan.mine + first) * HD, HD)
            for a in range(ref.shape[0]):
                target = targets[which + a].at[:, pl.ds(at, heads * HD)]
                copies.append(pltpu.make_async_copy(ref.at[a], target, sem.at[len(copies)]))
        for copy in copies:
            copy.start()
        for copy in copies:
            copy.wait()

    out = [shape(plan.slab, plan.groups * HD)] * 4
    return pl.pallas_call(
        body,
        out_shape=out,
        in_specs=[VMEM] * len(pieces) + [HBM] * len(outs),
        out_specs=[HBM] * 4,
        input_output_aliases={len(pieces) + n: n for n in range(len(outs))},
        scratch_shapes=[pltpu.SemaphoreType.DMA((4 * plan.on,))],
        compiler_params=pltpu.CompilerParams(vmem_limit_bytes=VMEM_LIMIT),
        cost_estimate=SMALL,
        name="place",
    )(*[p[-1] for p in pieces], *outs)


def take_in(arrays):
    def body(*refs):
        for n in range(len(arrays)):
            refs[len(arrays) + n][...] = refs[n][...]

    return call_mover(body, arrays, [shape(*a.shape) for a in arrays], "take_in", LARGE)


def chunk_list(plan):
    sizes = [2, 1, 1, 1] if plan.mine == 5 else [1] * plan.mine
    return [(sum(sizes[:n]), size) for n, size in enumerate(sizes)]


def fetch_list(chunks):
    if len(chunks) < 4:
        return chunks
    return [*chunks[:2], (chunks[2][0], sum(heads for _, heads in chunks[2:]))]


def after(arrays, others):
    if not others:
        return list(arrays)
    return list(lax.optimization_barrier((tuple(arrays), tuple(others)))[0])


class Queue:
    def __init__(self, plan, window):
        self.plan, self.window, self.results = plan, window, []

    def send(self, array, others=(), **steps):
        waits = list(others)
        if len(self.results) >= self.window:
            waits.append(self.results[-self.window])
        result = self.plan.send(after([array], waits)[0], **steps)
        self.results.append(result)
        return result


class Line:
    def __init__(self):
        self.last = ()

    def tie(self, arrays):
        return after(arrays, self.last)

    def ran(self, results):
        self.last = (results[-1],)
        return results


def local(queries, keys, values, out_grad, tile_mask):
    plan = Plan(*queries.shape, lax.axis_size("head"), lax.axis_size("frame"))
    chunks = chunk_list(plan)
    line, inward, outer, depth = Line(), Queue(plan, 2), Queue(plan, 3), Queue(plan, 3)
    spans = fetch_list(chunks)
    last = len(chunks) - 1
    arrays = (queries, out_grad, keys, values)
    blocks = [(s, first, heads) for first, heads in spans for s in range(1, plan.on)]
    early = [(0, *c) for c in chunks[:2]]
    packed = line.ran(pack_columns(plan, arrays, blocks + early))
    outgoing, own = packed[: len(blocks)], list(packed[len(blocks) :])
    received = []

    def fetch(n, waits=()):
        group = outgoing[n * (plan.on - 1) : (n + 1) * (plan.on - 1)]
        received.append([inward.send(a, waits, o_step=s) for s, a in enumerate(group, 1)])

    def others(n):
        first, heads = chunks[n]
        for got, (start, count) in zip(received, spans, strict=True):
            if start <= first and first + heads <= start + count:
                return [(a, (first - start) * HD) for a in got]

    def exchange(n, group, weight=SMALL, steps=plan.steps):
        heads = chunks[n][1]
        arrays = line.tie([array for array, _ in group])
        group = [(array, at) for array, (_, at) in zip(arrays, group, strict=True)]
        ready = line.ran(pack_heads(plan, group, heads * HD, steps, weight))
        moved = [depth.send(a, z_step=k) for k, a in zip(steps[1:], ready[1:], strict=True)]
        return [ready[0], *moved]

    def join(n):
        rows = [line.tie(arrived[n][0]), *arrived[n][1:]]
        orders = [plan.steps if n or m else plan.first_steps for m in range(len(rows))]
        qg, kv = line.ran(join_rows(plan, rows, chunks[n][1] * HD, orders))
        return qg, [kv] + [plan.send(kv, i_step=m) for m in range(1, plan.inn)]

    def work(n):
        first, heads = chunks[n]
        qg, kvs = joined[n]
        tied = line.tie([qg])[0]
        split = n == last
        results = line.ran(attend(plan, tile_mask, tied, kvs, first, heads, split))
        row_parts, key_parts = results[: plan.on], results[plan.on :]
        parts = [
            plan.send(a, i_step=(m + 1) // 2 if split else m, returning=True)
            for m, a in enumerate(key_parts)
            if m
        ]
        return row_parts, key_parts[0], parts

    def give_back(group):
        return [outer.send(a, o_step=s, returning=True) if s else a for s, a in enumerate(group)]

    def sums(n, row_parts, own, parts, together):
        width = chunks[n][1] * HD
        together = row_parts if together else []
        both = line.ran(add_parts(plan, line.tie([own])[0], parts, together, width))
        groups = [give_back(both)] if together else [row_parts, give_back(both)]
        return [(s, 2 * w, a) for w, group in enumerate(groups) for s, a in enumerate(group)]

    def put(n, pieces, outs):
        step, which, array = pieces[0]
        pieces = [(step, which, line.tie([array])[0]), *pieces[1:]]
        return line.ran(place(plan, pieces, *chunks[n], outs))

    arrived, joined, pieces, outs = [], [], [], []
    for n in range(min(2, len(spans))):
        fetch(n)
    arrived.append([exchange(0, [(own[0], 0)], steps=plan.first_steps)])
    if plan.on > 1:
        arrived[0].append(exchange(0, [(a, 0) for a in received[0]]))
    if last:
        arrived.append([exchange(1, [(own[1], 0), *others(1)])])
    joined.append(join(0))
    for n in range(2, len(spans)):
        fetch(n)
    for n in range(last):
        results = work(n)
        if n == 0 and last > 1:
            late = [(0, *c) for c in chunks[2:]]
            own += line.ran(pack_columns(plan, line.tie(arrays), late))
        if n >= 2:
            outs = put(n - 2, pieces[n - 2], outs)
        joined.append(join(n + 1))
        if n + 2 <= last:
            arrived.append([exchange(n + 2, [(own[n + 2], 0), *others(n + 2)], SMALL if n else LARGE)])
        if n and plan.on > 1:
            came = [piece for piece in pieces[n - 1] if piece[0]]
            copies = line.ran(take_in(line.tie([a for _, _, a in came])))
            kept = [piece for piece in pieces[n - 1] if not piece[0]]
            pieces[n - 1] = kept + [(s, w, a) for (s, w, _), a in zip(came, copies, strict=True)]
        pieces.append(sums(n, *results, True))
    row_parts, key_parts, parts = work(last)
    row_parts = give_back(row_parts)
    final = sums(last, row_parts, key_parts, parts, False)
    for n in range(max(0, last - 2), last):
        outs = put(n, pieces[n], outs)
    outs = put(last, final, outs)
    return tuple(outs)


def solution(mesh):
    rows = P(("dp", "frame", "head"), None)
    out = P(("dp", "frame"), "head")
    return jax.shard_map(
        local,
        mesh=mesh,
        in_specs=(rows, rows, rows, rows, P("head", None, None)),
        out_specs=(out, out, out, out),
        check_vma=False,
    )
```

```python
import functools
import math

import jax
import jax.numpy as jnp
from jax import lax
from jax.experimental import pallas as pl
from jax.experimental.pallas import tpu as pltpu
from jax.sharding import PartitionSpec as P

HD = 128
TILE = 128
EXCLUDED = -1e30
LOG2E = 1.4426950408889634
F32 = jnp.float32
BF16 = jnp.bfloat16
VMEM_LIMIT = 48 * 1024 * 1024
SMALL = pl.CostEstimate(flops=1024, bytes_accessed=1024, transcendentals=0)
LARGE = pl.CostEstimate(flops=1 << 33, bytes_accessed=1024, transcendentals=0)
HBM = pl.BlockSpec(memory_space=pltpu.HBM)
VMEM = pl.BlockSpec(memory_space=pltpu.VMEM)
SMEM = pl.BlockSpec(memory_space=pltpu.SMEM)


def there(index, step, size):
    if size & (size - 1) == 0:
        return index ^ step
    return (index + step) % size


def back(index, step, size):
    return there(index, step if size & (size - 1) == 0 else size - step, size)


class Plan:
    def __init__(self, rows, width, head_axis, frame_axis):
        self.rows = rows
        self.zn = head_axis
        far = [head_axis - 1, head_axis - 2] if head_axis > 2 else range(1, head_axis)
        self.steps = [0, *range(1, head_axis - 2), *far]
        self.first_steps = [0, *range(head_axis - 1, 0, -1)]
        self.groups = width // HD // head_axis
        self.on = math.gcd(self.groups, frame_axis)
        self.inn = frame_axis // self.on
        self.mine = self.groups // self.on
        self.slab = rows * head_axis
        self.tq = self.slab * self.on
        self.tk = self.tq * self.inn

    def place(self):
        frame = lax.axis_index("frame")
        return lax.axis_index("head"), frame // self.inn, frame % self.inn

    def column(self, z, o, first):
        return pl.multiple_of((z * self.groups + o * self.mine + first) * HD, HD)

    def send(self, array, z_step=0, o_step=0, i_step=0, returning=False):
        go = back if returning else there
        pairs = []
        for z in range(self.zn):
            for o in range(self.on):
                for i in range(self.inn):
                    source = (z * self.on + o) * self.inn + i
                    target = (
                        go(z, z_step, self.zn) * self.on + go(o, o_step, self.on)
                    ) * self.inn + go(i, i_step, self.inn)
                    pairs.append((source, target))
        return lax.ppermute(array, ("head", "frame"), pairs)


def shape(*dims, dtype=BF16):
    return jax.ShapeDtypeStruct(dims, dtype)


def call_mover(body, operands, out_shape, name, weight=SMALL):
    total = sum(math.prod(s.shape) * 2 for s in out_shape)
    return pl.pallas_call(
        body,
        out_shape=out_shape,
        in_specs=[VMEM] * len(operands),
        out_specs=[VMEM] * len(out_shape),
        compiler_params=pltpu.CompilerParams(vmem_limit_bytes=VMEM_LIMIT),
        cost_estimate=weight,
        name=name,
    )(*operands)


def pack_columns(plan, arrays, blocks):
    def body(*refs):
        ins, outs, held, sem = refs[:4], refs[4:-2], refs[-2], refs[-1]
        z, o, _ = plan.place()
        group = plan.groups * HD
        copies = []
        for k in range(plan.zn):
            at = pl.ds(pl.multiple_of(there(z, k, plan.zn) * group, HD), group)
            for a, ref in enumerate(ins):
                copies.append(
                    pltpu.make_async_copy(ref.at[:, at], held.at[k, a], sem.at[len(copies)])
                )
        for copy in copies:
            copy.start()
        for k in range(plan.zn):
            for copy in copies[4 * k : 4 * k + 4]:
                copy.wait()
            for out, (step, first, heads) in zip(outs, blocks, strict=True):
                at = pl.multiple_of((there(o, step, plan.on) * plan.mine + first) * HD, HD)
                out[k] = held[k, :, :, pl.ds(at, heads * HD)]

    out = [shape(plan.zn, 4, plan.rows, heads * HD) for _, _, heads in blocks]
    arrays = [pltpu.with_memory_space_constraint(a, pltpu.HBM) for a in arrays]
    return pl.pallas_call(
        body,
        out_shape=out,
        in_specs=[HBM] * 4,
        out_specs=[VMEM] * len(out),
        scratch_shapes=[
            pltpu.VMEM((plan.zn, 4, plan.rows, plan.groups * HD), BF16),
            pltpu.SemaphoreType.DMA((4 * plan.zn,)),
        ],
        compiler_params=pltpu.CompilerParams(vmem_limit_bytes=VMEM_LIMIT),
        cost_estimate=SMALL,
        name="pack_columns",
    )(*arrays)


def pack_heads(plan, groups, width, steps, weight=SMALL):
    def body(*refs):
        ins, outs = refs[: len(groups)], refs[len(groups) :]
        for k, out in zip(steps, outs, strict=True):
            for step, (ref, (_, at)) in enumerate(zip(ins, groups, strict=True)):
                out[step] = ref[k, :, :, at : at + width]

    out = [shape(len(groups), 4, plan.rows, width)] * plan.zn
    return call_mover(body, [array for array, _ in groups], out, "pack_heads", weight)


def join_rows(plan, sets, width, orders):
    def body(*refs):
        ins, (qg, kv) = refs[:-2], refs[-2:]
        z = lax.axis_index("head")
        for n, ref in enumerate(ins):
            start = sum(s[0].shape[0] for s in sets[: n // plan.zn])
            row = back(z, orders[n // plan.zn][n % plan.zn], plan.zn) * plan.rows
            for step in range(ref.shape[0]):
                at = (start + step) * plan.slab + row
                at = pl.ds(pl.multiple_of(at, plan.rows), plan.rows)
                for a in range(2):
                    qg[a, at], kv[a, at] = ref[step, a], ref[step, 2 + a]

    out = [shape(2, plan.tq, width)] * 2
    return call_mover(body, [a for s in sets for a in s], out, "join_rows")


def attend_body(plan, first, heads, split, *refs):
    mask, qg, kvs = refs[0], refs[1], refs[2 : 2 + plan.inn]
    rest = refs[2 + plan.inn :]
    row_outs, key_outs = rest[: plan.on], rest[plan.on : -7]
    key_t, value_t, scores, weights, grads, key_acc, value_acc = rest[-7:]
    _, o, i = plan.place()
    scaling = 1.0 / math.sqrt(HD)
    slab, tiles = plan.slab, plan.slab // TILE
    nt = (((1,), (1,)), ((), ()))
    dot = functools.partial(jnp.dot, preferred_element_type=F32)
    spots = [
        (m, step, t) for m in range(plan.inn) for step in range(plan.on) for t in range(tiles)
    ]

    def one_head(h, carry):
        cols = pl.ds(pl.multiple_of(h * HD, HD), HD)
        head = o * plan.mine + first + h
        for n, (m, step, t) in enumerate(spots):
            at = pl.ds(step * slab + t * TILE, TILE)
            put = pl.ds(n * TILE, TILE)
            key_t[:, put] = kvs[m][0, at, cols].astype(F32).T.astype(BF16)
            value_t[:, put] = kvs[m][1, at, cols].astype(F32).T.astype(BF16)

        for q_step in range(plan.on):
            q_at = pl.ds(q_step * slab, slab)
            q, g = qg[0, q_at, cols], qg[1, q_at, cols]
            q_tile = (back(o, q_step, plan.on) * plan.inn + i) * tiles
            peaks = [jnp.full((8, TILE), EXCLUDED, F32)] * tiles
            for n, (m, step, t) in enumerate(spots):
                key = kvs[m][0, pl.ds(step * slab + t * TILE, TILE), cols]
                k_tile = (back(o, step, plan.on) * plan.inn + back(i, m, plan.inn)) * tiles + t
                s = lax.dot_general(key, q, nt, preferred_element_type=F32) * (scaling * LOG2E)
                for j in range(tiles):
                    part = jnp.where(
                        mask[head, q_tile + j, k_tile] == 1,
                        s[:, j * TILE : (j + 1) * TILE],
                        EXCLUDED,
                    )
                    scores[pl.ds(n * TILE, TILE), pl.ds(j * TILE, TILE)] = part
                    peaks[j] = jnp.maximum(
                        peaks[j], jnp.max(part.reshape(TILE // 8, 8, TILE), axis=0)
                    )
            peak = jnp.concatenate([jnp.max(p, axis=0, keepdims=True) for p in peaks], axis=1)
            total = jnp.zeros((8, slab), F32)
            for n in range(len(spots)):
                at = pl.ds(n * TILE, TILE)
                w = jnp.exp2(scores[at] - peak)
                total += jnp.sum(w.reshape(TILE // 8, 8, slab), axis=0)
                scores[at] = w
                weights[at] = w.astype(BF16)
            inverse = 1.0 / jnp.sum(total, axis=0, keepdims=True)
            attended_t = (dot(value_t[...], weights[...]) * inverse).astype(BF16).astype(F32)
            delta = jnp.sum(g.astype(F32).T * attended_t, axis=0, keepdims=True)
            row_outs[q_step][0, :, cols] = attended_t.T.astype(BF16)
            for n, (m, step, t) in enumerate(spots):
                at = pl.ds(n * TILE, TILE)
                value = kvs[m][1, pl.ds(step * slab + t * TILE, TILE), cols]
                p = scores[at] * inverse
                dp = lax.dot_general(value, g, nt, preferred_element_type=F32)
                weights[at] = p.astype(BF16)
                grads[at] = (p * (dp - delta)).astype(BF16)
            query_t = dot(key_t[...], grads[...]) * scaling
            row_outs[q_step][1, :, cols] = query_t.T.astype(BF16)
            key_part, value_part = dot(grads[...], q), dot(weights[...], g)
            if q_step:
                key_part, value_part = key_part + key_acc[...], value_part + value_acc[...]
            if q_step < plan.on - 1:
                key_acc[...], value_acc[...] = key_part, value_part
            else:
                for m in range(plan.inn):
                    mine = slice(m * plan.tq, (m + 1) * plan.tq)
                    parts = (key_part[mine] * scaling, value_part[mine])
                    if m and split:
                        for out, part in zip(key_outs[2 * m - 1 : 2 * m + 1], parts, strict=True):
                            out[:, cols] = part.astype(out.dtype)
                    else:
                        out = key_outs[m]
                        out[0, :, cols] = parts[0].astype(out.dtype)
                        out[1, :, cols] = parts[1].astype(out.dtype)
        return carry

    lax.fori_loop(0, heads, one_head, 0)


def attend(plan, mask, qg, kvs, first, heads, split):
    width = heads * HD
    out = [shape(2, plan.slab, width)] * plan.on
    out += [shape(2, plan.tq, width, dtype=F32)]
    if split:
        out += [shape(plan.tq, width)] * (2 * plan.inn - 2)
    else:
        out += [shape(2, plan.tq, width)] * (plan.inn - 1)
    return pl.pallas_call(
        functools.partial(attend_body, plan, first, heads, split),
        out_shape=out,
        in_specs=[SMEM] + [VMEM] * (1 + plan.inn),
        out_specs=[VMEM] * len(out),
        scratch_shapes=[
            pltpu.VMEM((HD, plan.tk), BF16),
            pltpu.VMEM((HD, plan.tk), BF16),
            pltpu.VMEM((plan.tk, plan.slab), F32),
            pltpu.VMEM((plan.tk, plan.slab), BF16),
            pltpu.VMEM((plan.tk, plan.slab), BF16),
            pltpu.VMEM((plan.tk, HD), F32),
            pltpu.VMEM((plan.tk, HD), F32),
        ],
        compiler_params=pltpu.CompilerParams(vmem_limit_bytes=VMEM_LIMIT),
        cost_estimate=SMALL,
        name="attend",
    )(mask, qg, *kvs)


def add_parts(plan, own, parts, row_parts, width):
    def body(*refs):
        total = [refs[0][0], refs[0][1]]
        for n, ref in enumerate(refs[1 : 1 + len(parts)]):
            if len(ref.shape) == 2:
                total[n % 2] += ref[...].astype(F32)
            else:
                total = [part + ref[a].astype(F32) for a, part in enumerate(total)]
        rows = refs[1 + len(parts) : 1 + len(parts) + len(row_parts)]
        for step, out in enumerate(refs[1 + len(parts) + len(rows) :]):
            at = slice(step * plan.slab, (step + 1) * plan.slab)
            if rows:
                out[:2] = rows[step][...]
            for a, part in enumerate(total):
                out[2 * (len(rows) > 0) + a] = part[at].astype(BF16)

    return pl.pallas_call(
        body,
        out_shape=[shape(4 if row_parts else 2, plan.slab, width)] * plan.on,
        in_specs=[VMEM] * (1 + len(parts) + len(row_parts)),
        out_specs=[VMEM] * plan.on,
        compiler_params=pltpu.CompilerParams(vmem_limit_bytes=VMEM_LIMIT),
        cost_estimate=pl.CostEstimate(
            flops=2 * plan.tq * HD * len(parts),
            bytes_accessed=2 * plan.tq * HD * (8 + 2 * len(parts)),
            transcendentals=0,
        ),
        name="add_parts",
    )(own, *parts, *row_parts)


def place(plan, pieces, first, heads, outs):
    def body(*refs):
        ins, sem = refs[: len(pieces)], refs[-1]
        targets = refs[-5:-1]
        _, o, _ = plan.place()
        copies = []
        for ref, (step, which, _) in zip(ins, pieces, strict=True):
            at = pl.multiple_of((there(o, step, plan.on) * plan.mine + first) * HD, HD)
            for a in range(ref.shape[0]):
                target = targets[which + a].at[:, pl.ds(at, heads * HD)]
                copies.append(pltpu.make_async_copy(ref.at[a], target, sem.at[len(copies)]))
        for copy in copies:
            copy.start()
        for copy in copies:
            copy.wait()

    out = [shape(plan.slab, plan.groups * HD)] * 4
    return pl.pallas_call(
        body,
        out_shape=out,
        in_specs=[VMEM] * len(pieces) + [HBM] * len(outs),
        out_specs=[HBM] * 4,
        input_output_aliases={len(pieces) + n: n for n in range(len(outs))},
        scratch_shapes=[pltpu.SemaphoreType.DMA((4 * plan.on,))],
        compiler_params=pltpu.CompilerParams(vmem_limit_bytes=VMEM_LIMIT),
        cost_estimate=SMALL,
        name="place",
    )(*[p[-1] for p in pieces], *outs)


def take_in(arrays):
    def body(*refs):
        for n in range(len(arrays)):
            refs[len(arrays) + n][...] = refs[n][...]

    return call_mover(body, arrays, [shape(*a.shape) for a in arrays], "take_in", LARGE)


def chunk_list(plan):
    sizes = [2] + [1] * (plan.mine - 2) if plan.mine > 2 else [1] * plan.mine
    return [(sum(sizes[:n]), size) for n, size in enumerate(sizes)]


def fetch_list(chunks):
    if len(chunks) < 4:
        return chunks
    return [*chunks[:2], (chunks[2][0], sum(heads for _, heads in chunks[2:]))]


def after(arrays, others):
    if not others:
        return list(arrays)
    return list(lax.optimization_barrier((tuple(arrays), tuple(others)))[0])


class Queue:
    def __init__(self, plan, window):
        self.plan, self.window, self.results = plan, window, []

    def send(self, array, others=(), **steps):
        waits = list(others)
        if len(self.results) >= self.window:
            waits.append(self.results[-self.window])
        result = self.plan.send(after([array], waits)[0], **steps)
        self.results.append(result)
        return result


class Line:
    def __init__(self):
        self.last = ()

    def tie(self, arrays):
        return after(arrays, self.last)

    def ran(self, results):
        self.last = (results[-1],)
        return results


def local(queries, keys, values, out_grad, tile_mask):
    plan = Plan(*queries.shape, lax.axis_size("head"), lax.axis_size("frame"))
    chunks = chunk_list(plan)
    line, inward, outer, depth = Line(), Queue(plan, 2), Queue(plan, 3), Queue(plan, 3)
    spans = fetch_list(chunks)
    last = len(chunks) - 1
    arrays = (queries, out_grad, keys, values)
    blocks = [(s, first, heads) for first, heads in spans for s in range(1, plan.on)]
    early = [(0, *c) for c in chunks[:2]]
    packed = line.ran(pack_columns(plan, arrays, blocks + early))
    outgoing, own = packed[: len(blocks)], list(packed[len(blocks) :])
    received = []

    def fetch(n, waits=()):
        group = outgoing[n * (plan.on - 1) : (n + 1) * (plan.on - 1)]
        received.append([inward.send(a, waits, o_step=s) for s, a in enumerate(group, 1)])

    def others(n):
        first, heads = chunks[n]
        for got, (start, count) in zip(received, spans, strict=True):
            if start <= first and first + heads <= start + count:
                return [(a, (first - start) * HD) for a in got]

    def exchange(n, group, weight=SMALL, steps=plan.steps):
        heads = chunks[n][1]
        arrays = line.tie([array for array, _ in group])
        group = [(array, at) for array, (_, at) in zip(arrays, group, strict=True)]
        ready = line.ran(pack_heads(plan, group, heads * HD, steps, weight))
        moved = [depth.send(a, z_step=k) for k, a in zip(steps[1:], ready[1:], strict=True)]
        return [ready[0], *moved]

    def join(n):
        rows = [line.tie(arrived[n][0]), *arrived[n][1:]]
        orders = [plan.steps if n or m else plan.first_steps for m in range(len(rows))]
        qg, kv = line.ran(join_rows(plan, rows, chunks[n][1] * HD, orders))
        return qg, [kv] + [plan.send(kv, i_step=m) for m in range(1, plan.inn)]

    def work(n):
        first, heads = chunks[n]
        qg, kvs = joined[n]
        tied = line.tie([qg])[0]
        split = n == last
        results = line.ran(attend(plan, tile_mask, tied, kvs, first, heads, split))
        row_parts, key_parts = results[: plan.on], results[plan.on :]
        parts = [
            plan.send(a, i_step=(m + 1) // 2 if split else m, returning=True)
            for m, a in enumerate(key_parts)
            if m
        ]
        return row_parts, key_parts[0], parts

    def give_back(group):
        return [outer.send(a, o_step=s, returning=True) if s else a for s, a in enumerate(group)]

    def sums(n, row_parts, own, parts, together):
        width = chunks[n][1] * HD
        together = row_parts if together else []
        both = line.ran(add_parts(plan, line.tie([own])[0], parts, together, width))
        groups = [give_back(both)] if together else [row_parts, give_back(both)]
        return [(s, 2 * w, a) for w, group in enumerate(groups) for s, a in enumerate(group)]

    def put(n, pieces, outs):
        step, which, array = pieces[0]
        pieces = [(step, which, line.tie([array])[0]), *pieces[1:]]
        return line.ran(place(plan, pieces, *chunks[n], outs))

    arrived, joined, pieces, outs = [], [], [], []
    for n in range(min(2, len(spans))):
        fetch(n)
    arrived.append([exchange(0, [(own[0], 0)], steps=plan.first_steps)])
    if plan.on > 1:
        arrived[0].append(exchange(0, [(a, 0) for a in received[0]]))
    if last:
        arrived.append([exchange(1, [(own[1], 0), *others(1)])])
    joined.append(join(0))
    for n in range(2, len(spans)):
        fetch(n)
    for n in range(last):
        results = work(n)
        if n == 0 and last > 1:
            late = [(0, *c) for c in chunks[2:]]
            own += line.ran(pack_columns(plan, line.tie(arrays), late))
        if n >= 2:
            outs = put(n - 2, pieces[n - 2], outs)
        joined.append(join(n + 1))
        if n + 2 <= last:
            arrived.append([exchange(n + 2, [(own[n + 2], 0), *others(n + 2)], SMALL if n else LARGE)])
        if n and plan.on > 1:
            came = [piece for piece in pieces[n - 1] if piece[0]]
            copies = line.ran(take_in(line.tie([a for _, _, a in came])))
            kept = [piece for piece in pieces[n - 1] if not piece[0]]
            pieces[n - 1] = kept + [(s, w, a) for (s, w, _), a in zip(came, copies, strict=True)]
        pieces.append(sums(n, *results, True))
    row_parts, key_parts, parts = work(last)
    row_parts = give_back(row_parts)
    final = sums(last, row_parts, key_parts, parts, False)
    for n in range(max(0, last - 2), last):
        outs = put(n, pieces[n], outs)
    late = [piece for piece in final if piece[0] and piece[1]]
    outs = put(last, [piece for piece in final if not (piece[0] and piece[1])], outs)
    if late:
        outs = put(last, late, outs)
    return tuple(outs)


def solution(mesh):
    rows = P(("dp", "frame", "head"), None)
    out = P(("dp", "frame"), "head")
    return jax.shard_map(
        local,
        mesh=mesh,
        in_specs=(rows, rows, rows, rows, P("head", None, None)),
        out_specs=(out, out, out, out),
        check_vma=False,
    )
```

```python
import functools
import math

import jax
import jax.numpy as jnp
from jax import lax
from jax.experimental import pallas as pl
from jax.experimental.pallas import tpu as pltpu
from jax.sharding import PartitionSpec as P

HD = 128
TILE = 128
EXCLUDED = -1e30
LOG2E = 1.4426950408889634
F32 = jnp.float32
BF16 = jnp.bfloat16
VMEM_LIMIT = 48 * 1024 * 1024
SMALL = pl.CostEstimate(flops=1024, bytes_accessed=1024, transcendentals=0)
LARGE = pl.CostEstimate(flops=1 << 33, bytes_accessed=1024, transcendentals=0)
HBM = pl.BlockSpec(memory_space=pltpu.HBM)
VMEM = pl.BlockSpec(memory_space=pltpu.VMEM)
SMEM = pl.BlockSpec(memory_space=pltpu.SMEM)


def there(index, step, size):
    if size & (size - 1) == 0:
        return index ^ step
    return (index + step) % size


def back(index, step, size):
    return there(index, step if size & (size - 1) == 0 else size - step, size)


class Plan:
    def __init__(self, rows, width, head_axis, frame_axis):
        self.rows = rows
        self.zn = head_axis
        far = [head_axis - 1, head_axis - 2] if head_axis > 2 else range(1, head_axis)
        self.steps = [0, *range(1, head_axis - 2), *far]
        self.first_steps = [0, *range(head_axis - 1, 0, -1)]
        self.groups = width // HD // head_axis
        self.on = math.gcd(self.groups, frame_axis)
        self.inn = frame_axis // self.on
        self.mine = self.groups // self.on
        self.slab = rows * head_axis
        self.tq = self.slab * self.on
        self.tk = self.tq * self.inn

    def place(self):
        frame = lax.axis_index("frame")
        return lax.axis_index("head"), frame // self.inn, frame % self.inn

    def column(self, z, o, first):
        return pl.multiple_of((z * self.groups + o * self.mine + first) * HD, HD)

    def send(self, array, z_step=0, o_step=0, i_step=0, returning=False):
        go = back if returning else there
        pairs = []
        for z in range(self.zn):
            for o in range(self.on):
                for i in range(self.inn):
                    source = (z * self.on + o) * self.inn + i
                    target = (
                        go(z, z_step, self.zn) * self.on + go(o, o_step, self.on)
                    ) * self.inn + go(i, i_step, self.inn)
                    pairs.append((source, target))
        return lax.ppermute(array, ("head", "frame"), pairs)


def shape(*dims, dtype=BF16):
    return jax.ShapeDtypeStruct(dims, dtype)


def call_mover(body, operands, out_shape, name, weight=SMALL):
    total = sum(math.prod(s.shape) * 2 for s in out_shape)
    return pl.pallas_call(
        body,
        out_shape=out_shape,
        in_specs=[VMEM] * len(operands),
        out_specs=[VMEM] * len(out_shape),
        compiler_params=pltpu.CompilerParams(vmem_limit_bytes=VMEM_LIMIT),
        cost_estimate=weight,
        name=name,
    )(*operands)


def pack_columns(plan, arrays, blocks):
    def body(*refs):
        ins, outs, held, sem = refs[:4], refs[4:-2], refs[-2], refs[-1]
        z, o, _ = plan.place()
        group = plan.groups * HD
        copies = []
        for k in range(plan.zn):
            at = pl.ds(pl.multiple_of(there(z, k, plan.zn) * group, HD), group)
            for a, ref in enumerate(ins):
                copies.append(
                    pltpu.make_async_copy(ref.at[:, at], held.at[k, a], sem.at[len(copies)])
                )
        for copy in copies:
            copy.start()
        for k in range(plan.zn):
            for copy in copies[4 * k : 4 * k + 4]:
                copy.wait()
            for out, (step, first, heads) in zip(outs, blocks, strict=True):
                at = pl.multiple_of((there(o, step, plan.on) * plan.mine + first) * HD, HD)
                out[k] = held[k, :, :, pl.ds(at, heads * HD)]

    out = [shape(plan.zn, 4, plan.rows, heads * HD) for _, _, heads in blocks]
    arrays = [pltpu.with_memory_space_constraint(a, pltpu.HBM) for a in arrays]
    return pl.pallas_call(
        body,
        out_shape=out,
        in_specs=[HBM] * 4,
        out_specs=[VMEM] * len(out),
        scratch_shapes=[
            pltpu.VMEM((plan.zn, 4, plan.rows, plan.groups * HD), BF16),
            pltpu.SemaphoreType.DMA((4 * plan.zn,)),
        ],
        compiler_params=pltpu.CompilerParams(vmem_limit_bytes=VMEM_LIMIT),
        cost_estimate=SMALL,
        name="pack_columns",
    )(*arrays)


def pack_heads(plan, groups, width, steps, weight=SMALL):
    def body(*refs):
        ins, outs = refs[: len(groups)], refs[len(groups) :]
        for k, out in zip(steps, outs, strict=True):
            for step, (ref, (_, at)) in enumerate(zip(ins, groups, strict=True)):
                out[step] = ref[k, :, :, at : at + width]

    out = [shape(len(groups), 4, plan.rows, width)] * plan.zn
    return call_mover(body, [array for array, _ in groups], out, "pack_heads", weight)


def join_rows(plan, sets, width, orders):
    def body(*refs):
        ins, (qg, kv) = refs[:-2], refs[-2:]
        z = lax.axis_index("head")
        for n, ref in enumerate(ins):
            start = sum(s[0].shape[0] for s in sets[: n // plan.zn])
            row = back(z, orders[n // plan.zn][n % plan.zn], plan.zn) * plan.rows
            for step in range(ref.shape[0]):
                at = (start + step) * plan.slab + row
                at = pl.ds(pl.multiple_of(at, plan.rows), plan.rows)
                for a in range(2):
                    qg[a, at], kv[a, at] = ref[step, a], ref[step, 2 + a]

    out = [shape(2, plan.tq, width)] * 2
    return call_mover(body, [a for s in sets for a in s], out, "join_rows")


def attend_body(plan, first, heads, split, *refs):
    mask, qg, kvs = refs[0], refs[1], refs[2 : 2 + plan.inn]
    rest = refs[2 + plan.inn :]
    row_outs, key_outs = rest[: plan.on], rest[plan.on : -7]
    key_t, value_t, scores, weights, grads, key_acc, value_acc = rest[-7:]
    _, o, i = plan.place()
    scaling = 1.0 / math.sqrt(HD)
    slab, tiles = plan.slab, plan.slab // TILE
    nt = (((1,), (1,)), ((), ()))
    dot = functools.partial(jnp.dot, preferred_element_type=F32)
    spots = [
        (m, step, t) for m in range(plan.inn) for step in range(plan.on) for t in range(tiles)
    ]

    def one_head(h, carry):
        cols = pl.ds(pl.multiple_of(h * HD, HD), HD)
        head = o * plan.mine + first + h
        for n, (m, step, t) in enumerate(spots):
            at = pl.ds(step * slab + t * TILE, TILE)
            put = pl.ds(n * TILE, TILE)
            key_t[:, put] = kvs[m][0, at, cols].astype(F32).T.astype(BF16)
            value_t[:, put] = kvs[m][1, at, cols].astype(F32).T.astype(BF16)

        for q_step in range(plan.on):
            q_at = pl.ds(q_step * slab, slab)
            q, g = qg[0, q_at, cols], qg[1, q_at, cols]
            q_tile = (back(o, q_step, plan.on) * plan.inn + i) * tiles
            peaks = [jnp.full((8, TILE), EXCLUDED, F32)] * tiles
            for n, (m, step, t) in enumerate(spots):
                key = kvs[m][0, pl.ds(step * slab + t * TILE, TILE), cols]
                k_tile = (back(o, step, plan.on) * plan.inn + back(i, m, plan.inn)) * tiles + t
                s = lax.dot_general(key, q, nt, preferred_element_type=F32) * (scaling * LOG2E)
                for j in range(tiles):
                    part = jnp.where(
                        mask[head, q_tile + j, k_tile] == 1,
                        s[:, j * TILE : (j + 1) * TILE],
                        EXCLUDED,
                    )
                    scores[pl.ds(n * TILE, TILE), pl.ds(j * TILE, TILE)] = part
                    peaks[j] = jnp.maximum(
                        peaks[j], jnp.max(part.reshape(TILE // 8, 8, TILE), axis=0)
                    )
            peak = jnp.concatenate([jnp.max(p, axis=0, keepdims=True) for p in peaks], axis=1)
            total = jnp.zeros((8, slab), F32)
            for n in range(len(spots)):
                at = pl.ds(n * TILE, TILE)
                w = jnp.exp2(scores[at] - peak)
                total += jnp.sum(w.reshape(TILE // 8, 8, slab), axis=0)
                scores[at] = w
                weights[at] = w.astype(BF16)
            inverse = 1.0 / jnp.sum(total, axis=0, keepdims=True)
            attended_t = (dot(value_t[...], weights[...]) * inverse).astype(BF16).astype(F32)
            delta = jnp.sum(g.astype(F32).T * attended_t, axis=0, keepdims=True)
            row_outs[q_step][0, :, cols] = attended_t.T.astype(BF16)
            for n, (m, step, t) in enumerate(spots):
                at = pl.ds(n * TILE, TILE)
                value = kvs[m][1, pl.ds(step * slab + t * TILE, TILE), cols]
                p = scores[at] * inverse
                dp = lax.dot_general(value, g, nt, preferred_element_type=F32)
                weights[at] = p.astype(BF16)
                grads[at] = (p * (dp - delta)).astype(BF16)
            query_t = dot(key_t[...], grads[...]) * scaling
            row_outs[q_step][1, :, cols] = query_t.T.astype(BF16)
            key_part, value_part = dot(grads[...], q), dot(weights[...], g)
            if q_step:
                key_part, value_part = key_part + key_acc[...], value_part + value_acc[...]
            if q_step < plan.on - 1:
                key_acc[...], value_acc[...] = key_part, value_part
            else:
                for m in range(plan.inn):
                    mine = slice(m * plan.tq, (m + 1) * plan.tq)
                    parts = (key_part[mine] * scaling, value_part[mine])
                    if m and split:
                        for out, part in zip(key_outs[2 * m - 1 : 2 * m + 1], parts, strict=True):
                            out[:, cols] = part.astype(out.dtype)
                    else:
                        out = key_outs[m]
                        out[0, :, cols] = parts[0].astype(out.dtype)
                        out[1, :, cols] = parts[1].astype(out.dtype)
        return carry

    lax.fori_loop(0, heads, one_head, 0)


def attend(plan, mask, qg, kvs, first, heads, split):
    width = heads * HD
    out = [shape(2, plan.slab, width)] * plan.on
    out += [shape(2, plan.tq, width, dtype=F32)]
    if split:
        out += [shape(plan.tq, width)] * (2 * plan.inn - 2)
    else:
        out += [shape(2, plan.tq, width)] * (plan.inn - 1)
    return pl.pallas_call(
        functools.partial(attend_body, plan, first, heads, split),
        out_shape=out,
        in_specs=[SMEM] + [VMEM] * (1 + plan.inn),
        out_specs=[VMEM] * len(out),
        scratch_shapes=[
            pltpu.VMEM((HD, plan.tk), BF16),
            pltpu.VMEM((HD, plan.tk), BF16),
            pltpu.VMEM((plan.tk, plan.slab), F32),
            pltpu.VMEM((plan.tk, plan.slab), BF16),
            pltpu.VMEM((plan.tk, plan.slab), BF16),
            pltpu.VMEM((plan.tk, HD), F32),
            pltpu.VMEM((plan.tk, HD), F32),
        ],
        compiler_params=pltpu.CompilerParams(vmem_limit_bytes=VMEM_LIMIT),
        cost_estimate=SMALL,
        name="attend",
    )(mask, qg, *kvs)


def add_parts(plan, own, parts, row_parts, width):
    def body(*refs):
        total = [refs[0][0], refs[0][1]]
        for n, ref in enumerate(refs[1 : 1 + len(parts)]):
            if len(ref.shape) == 2:
                total[n % 2] += ref[...].astype(F32)
            else:
                total = [part + ref[a].astype(F32) for a, part in enumerate(total)]
        rows = refs[1 + len(parts) : 1 + len(parts) + len(row_parts)]
        for step, out in enumerate(refs[1 + len(parts) + len(rows) :]):
            at = slice(step * plan.slab, (step + 1) * plan.slab)
            if rows:
                out[:2] = rows[step][...]
            for a, part in enumerate(total):
                out[2 * (len(rows) > 0) + a] = part[at].astype(BF16)

    return pl.pallas_call(
        body,
        out_shape=[shape(4 if row_parts else 2, plan.slab, width)] * plan.on,
        in_specs=[VMEM] * (1 + len(parts) + len(row_parts)),
        out_specs=[VMEM] * plan.on,
        compiler_params=pltpu.CompilerParams(vmem_limit_bytes=VMEM_LIMIT),
        cost_estimate=pl.CostEstimate(
            flops=2 * plan.tq * HD * len(parts),
            bytes_accessed=2 * plan.tq * HD * (8 + 2 * len(parts)),
            transcendentals=0,
        ),
        name="add_parts",
    )(own, *parts, *row_parts)


def place(plan, pieces, first, heads, outs):
    def body(*refs):
        ins, sem = refs[: len(pieces)], refs[-1]
        targets = refs[-5:-1]
        _, o, _ = plan.place()
        copies = []
        for ref, (step, which, _) in zip(ins, pieces, strict=True):
            at = pl.multiple_of((there(o, step, plan.on) * plan.mine + first) * HD, HD)
            for a in range(ref.shape[0]):
                target = targets[which + a].at[:, pl.ds(at, heads * HD)]
                copies.append(pltpu.make_async_copy(ref.at[a], target, sem.at[len(copies)]))
        for copy in copies:
            copy.start()
        for copy in copies:
            copy.wait()

    out = [shape(plan.slab, plan.groups * HD)] * 4
    return pl.pallas_call(
        body,
        out_shape=out,
        in_specs=[VMEM] * len(pieces) + [HBM] * len(outs),
        out_specs=[HBM] * 4,
        input_output_aliases={len(pieces) + n: n for n in range(len(outs))},
        scratch_shapes=[pltpu.SemaphoreType.DMA((8 * plan.on,))],
        compiler_params=pltpu.CompilerParams(vmem_limit_bytes=VMEM_LIMIT),
        cost_estimate=SMALL,
        name="place",
    )(*[p[-1] for p in pieces], *outs)


def take_in(arrays):
    def body(*refs):
        for n in range(len(arrays)):
            refs[len(arrays) + n][...] = refs[n][...]

    return call_mover(body, arrays, [shape(*a.shape) for a in arrays], "take_in", LARGE)


def chunk_list(plan):
    sizes = [2] + [1] * (plan.mine - 2) if plan.mine > 2 else [1] * plan.mine
    return [(sum(sizes[:n]), size) for n, size in enumerate(sizes)]


def fetch_list(chunks):
    if len(chunks) < 4:
        return chunks
    return [*chunks[:2], (chunks[2][0], sum(heads for _, heads in chunks[2:]))]


def after(arrays, others):
    if not others:
        return list(arrays)
    return list(lax.optimization_barrier((tuple(arrays), tuple(others)))[0])


class Queue:
    def __init__(self, plan, window):
        self.plan, self.window, self.results = plan, window, []

    def send(self, array, others=(), **steps):
        waits = list(others)
        if len(self.results) >= self.window:
            waits.append(self.results[-self.window])
        result = self.plan.send(after([array], waits)[0], **steps)
        self.results.append(result)
        return result


class Line:
    def __init__(self):
        self.last = ()

    def tie(self, arrays):
        return after(arrays, self.last)

    def ran(self, results):
        self.last = (results[-1],)
        return results


def local(queries, keys, values, out_grad, tile_mask):
    plan = Plan(*queries.shape, lax.axis_size("head"), lax.axis_size("frame"))
    chunks = chunk_list(plan)
    line, inward, outer, depth = Line(), Queue(plan, 2), Queue(plan, 3), Queue(plan, 3)
    spans = fetch_list(chunks)
    last = len(chunks) - 1
    arrays = (queries, out_grad, keys, values)
    blocks = [(s, first, heads) for first, heads in spans for s in range(1, plan.on)]
    early = [(0, *c) for c in chunks[:2]]
    packed = line.ran(pack_columns(plan, arrays, blocks + early))
    outgoing, own = packed[: len(blocks)], list(packed[len(blocks) :])
    received = []

    def fetch(n, waits=()):
        group = outgoing[n * (plan.on - 1) : (n + 1) * (plan.on - 1)]
        received.append([inward.send(a, waits, o_step=s) for s, a in enumerate(group, 1)])

    def others(n):
        first, heads = chunks[n]
        for got, (start, count) in zip(received, spans, strict=True):
            if start <= first and first + heads <= start + count:
                return [(a, (first - start) * HD) for a in got]

    def exchange(n, group, weight=SMALL, steps=plan.steps):
        heads = chunks[n][1]
        arrays = line.tie([array for array, _ in group])
        group = [(array, at) for array, (_, at) in zip(arrays, group, strict=True)]
        ready = line.ran(pack_heads(plan, group, heads * HD, steps, weight))
        moved = [depth.send(a, z_step=k) for k, a in zip(steps[1:], ready[1:], strict=True)]
        return [ready[0], *moved]

    def join(n):
        rows = [line.tie(arrived[n][0]), *arrived[n][1:]]
        orders = [plan.steps if n or m else plan.first_steps for m in range(len(rows))]
        qg, kv = line.ran(join_rows(plan, rows, chunks[n][1] * HD, orders))
        return qg, [kv] + [plan.send(kv, i_step=m) for m in range(1, plan.inn)]

    def work(n):
        first, heads = chunks[n]
        qg, kvs = joined[n]
        tied = line.tie([qg])[0]
        split = n == last
        results = line.ran(attend(plan, tile_mask, tied, kvs, first, heads, split))
        row_parts, key_parts = results[: plan.on], results[plan.on :]
        parts = [
            plan.send(a, i_step=(m + 1) // 2 if split else m, returning=True)
            for m, a in enumerate(key_parts)
            if m
        ]
        return row_parts, key_parts[0], parts

    def give_back(group):
        return [outer.send(a, o_step=s, returning=True) if s else a for s, a in enumerate(group)]

    def sums(n, row_parts, own, parts, together):
        width = chunks[n][1] * HD
        together = row_parts if together else []
        both = line.ran(add_parts(plan, line.tie([own])[0], parts, together, width))
        groups = [give_back(both)] if together else [row_parts, give_back(both)]
        return [(s, 2 * w, a) for w, group in enumerate(groups) for s, a in enumerate(group)]

    def put(n, pieces, outs):
        step, which, array = pieces[0]
        pieces = [(step, which, line.tie([array])[0]), *pieces[1:]]
        return line.ran(place(plan, pieces, *chunks[n], outs))

    arrived, joined, pieces, outs = [], [], [], []
    for n in range(min(2, len(spans))):
        fetch(n)
    arrived.append([exchange(0, [(own[0], 0)], steps=plan.first_steps)])
    if plan.on > 1:
        arrived[0].append(exchange(0, [(a, 0) for a in received[0]]))
    if last:
        arrived.append([exchange(1, [(own[1], 0), *others(1)])])
    joined.append(join(0))
    for n in range(2, len(spans)):
        fetch(n)
    for n in range(last):
        results = work(n)
        if n == 0 and last > 1:
            late = [(0, *c) for c in chunks[2:]]
            own += line.ran(pack_columns(plan, line.tie(arrays), late))
        if n >= 2:
            outs = put(n - 2, pieces[n - 2], outs)
        joined.append(join(n + 1))
        if n + 2 <= last:
            arrived.append([exchange(n + 2, [(own[n + 2], 0), *others(n + 2)], SMALL if n else LARGE)])
        if n and plan.on > 1:
            came = [piece for piece in pieces[n - 1] if piece[0]]
            copies = line.ran(take_in(line.tie([a for _, _, a in came])))
            kept = [piece for piece in pieces[n - 1] if not piece[0]]
            pieces[n - 1] = kept + [(s, w, a) for (s, w, _), a in zip(came, copies, strict=True)]
        if n == last - 2:
            row_parts, key_parts, parts = results
            pieces.append(sums(n, give_back(row_parts), key_parts, parts, False))
        else:
            pieces.append(sums(n, *results, True))
    row_parts, key_parts, parts = work(last)
    row_parts = give_back(row_parts)
    final = sums(last, row_parts, key_parts, parts, False)
    for n in range(max(0, last - 2), last):
        outs = put(n, pieces[n], outs)
    late = [piece for piece in final if piece[0] and piece[1]]
    outs = put(last, [piece for piece in final if not (piece[0] and piece[1])], outs)
    if late:
        outs = put(last, late, outs)
    return tuple(outs)


def solution(mesh):
    rows = P(("dp", "frame", "head"), None)
    out = P(("dp", "frame"), "head")
    return jax.shard_map(
        local,
        mesh=mesh,
        in_specs=(rows, rows, rows, rows, P("head", None, None)),
        out_specs=(out, out, out, out),
        check_vma=False,
    )
```
